128 devices in a mesh: dp: 4 (over y_hi, core), cent: 32 (over z, x, y_lo).
Axes of the slice: x: 4, y: 4 (y_hi: 2, y_lo: 2; y = y_hi * 2 + y_lo), z: 4, core: 2. Of those that a mesh axis runs over, the one named last changes fastest.
Arguments:
- points: bfloat16 [8192, 1024], P(('dp', 'cent')), may hold values from -100 to 100
- centroids: bfloat16 [50176, 1024], P('cent'), may hold values from -8 to 8
Outputs:
- new_centroids: bfloat16 [50176, 1024], P('cent', 'dp')
- log_partition: float32 [8192], P(('dp', 'cent'))
The draws below stay inside these ranges and needn't reach their ends.
All inputs are finite; a program needn't handle non-finite values.
Results may differ from the reference program's by a relative error of at most 0.0024.
Values may be sent and summed in bfloat16 or wider, within the bound.
No kernel may reach another device: no remote copies, remote signals or barrier semaphores. Data moves between devices by JAX's collectives and lax.ppermute only.
A program may use at most 128 MiB of HBM per device.

```python
import jax
import jax.numpy as jnp
from jax import lax

D = 1024
K_DEV = 1568
K = 50176
PTS = 8192
N_CENT = 32


def shared_base(key):
    return jnp.clip(jax.random.normal(key, (K, D), jnp.float32), -6.0, 6.0)


def twin_centroids(key, spread):
    base = shared_base(key)
    noise = jax.random.normal(jax.random.fold_in(key, 11), (K, D), jnp.float32)
    twin = jnp.clip(jnp.roll(base, 1, axis=0) + spread * noise, -7.5, 7.5)
    marked = jnp.arange(K) % (K // 8) == 1
    return jnp.where(marked[:, None], twin, base)


def draw_centroids(key, part):
    base = twin_centroids(key, 0.2)
    return base.astype(jnp.bfloat16)


def draw_points(key, part):
    base = shared_base(key)
    key = jax.random.fold_in(key, 7)
    values = jnp.clip(jax.random.normal(key, (PTS, D), jnp.float32), -6.0, 6.0)
    anchors = base[::K // 8][:8]
    anchor_norm = jnp.sum(anchors * anchors, axis=1)
    rows = jnp.arange(PTS)
    pick = jnp.minimum(rows // (PTS // 8), 7)
    level = jnp.array([110.0, 160.0, 220.0], jnp.float32)[pick % 3]
    factor = 0.5 + level * D ** 0.5 / (2.0 * jnp.take(anchor_norm, pick))
    chosen = jnp.take(anchors, pick, axis=0) * factor[:, None]
    marked = rows % (PTS // 8) == 0
    values = jnp.where(marked[:, None], chosen, values)
    return values.astype(jnp.bfloat16)


def setup_inputs(seed: int = 0) -> dict:
    key_list = jax.random.split(jax.random.key(seed), 3)
    return {
        "points": draw_points(jax.random.fold_in(key_list[2], 71), 0),
        "centroids": draw_centroids(jax.random.fold_in(key_list[2], 71), 0),
    }


def reference(points, centroids):
    scale = 1.0 / (D ** 0.5)
    blocks = centroids.reshape(N_CENT, K_DEV, D)

    def block_logits(block):
        cnorm = jnp.sum(jnp.square(block.astype(jnp.float32)), axis=1)
        cross = jnp.dot(points, block.T, preferred_element_type=jnp.float32)
        return (2.0 * cross - cnorm[None, :]) * scale

    def first_pass(carry, block):
        run_max, run_total = carry
        logits = block_logits(block)
        new_max = jnp.maximum(run_max, jnp.max(logits, axis=1))
        run_total = run_total * jnp.exp(run_max - new_max) + jnp.sum(jnp.exp(logits - new_max[:, None]), axis=1)
        return (new_max, run_total), None

    start = (jnp.full((PTS,), -jnp.inf, jnp.float32), jnp.zeros((PTS,), jnp.float32))
    (row_max, total), _ = lax.scan(first_pass, start, blocks)
    log_partition = row_max + jnp.log(total)

    def second_pass(carry, block):
        logits = block_logits(block)
        resp = (jnp.exp(logits - row_max[:, None]) / total[:, None]).astype(jnp.bfloat16)
        sums = jnp.dot(resp.T, points, preferred_element_type=jnp.float32)
        counts = jnp.sum(resp.astype(jnp.float32), axis=0)
        fresh = (sums + 0.25 * block.astype(jnp.float32)) / (counts[:, None] + 0.25)
        return carry, fresh.astype(jnp.bfloat16)

    _, fresh = lax.scan(second_pass, jnp.zeros((), jnp.float32), blocks)
    return fresh.reshape(K, D), log_partition
```

```python
import functools

import jax
import jax.numpy as jnp
from jax import lax
from jax.experimental import pallas as pl
from jax.experimental.pallas import tpu as pltpu
from jax.sharding import PartitionSpec as P

D = 1024
PTS_DEV = 64
N_CENT = 32
K_DEV = 1568
ROWS = PTS_DEV * N_CENT
WIDTH = D // 4
SCALE = 1.0 / D**0.5
VMEM = 56 * 1024 * 1024
SPAN = 256.0


def logits_body(sub, cent, cnorm, pts, logits, stats):
    p = pts[...]
    top, total = None, None
    for j in range(K_DEV // sub):
        rows = slice(j * sub, (j + 1) * sub)
        cross = lax.dot_general(
            cent[rows, :], p, (((1,), (1,)), ((), ())), preferred_element_type=jnp.float32
        )
        part = (2.0 * cross - cnorm[rows, :]) * SCALE
        logits[rows, :] = part
        part_top = jnp.max(part, axis=0, keepdims=True)
        new_top = part_top if top is None else jnp.maximum(top, part_top)
        part_total = jnp.sum(jnp.exp(part - new_top), axis=0, keepdims=True)
        total = part_total if top is None else total * jnp.exp(top - new_top) + part_total
        top = new_top
    stats[0:1, :] = top
    stats[1:2, :] = total


def local_logits(centroids, cnorm, points, tile=512, sub=784):
    rows = points.shape[0]
    return pl.pallas_call(
        functools.partial(logits_body, sub),
        grid=(rows // tile,),
        in_specs=[
            pl.BlockSpec((K_DEV, D), lambda i: (0, 0)),
            pl.BlockSpec((K_DEV, 1), lambda i: (0, 0)),
            pl.BlockSpec((tile, D), lambda i: (i, 0)),
        ],
        out_specs=[
            pl.BlockSpec((K_DEV, tile), lambda i: (0, i)),
            pl.BlockSpec((2, tile), lambda i: (0, i)),
        ],
        out_shape=[
            jax.ShapeDtypeStruct((K_DEV, rows), jnp.float32),
            jax.ShapeDtypeStruct((2, rows), jnp.float32),
        ],
        compiler_params=pltpu.CompilerParams(vmem_limit_bytes=VMEM),
        name="logits",
    )(centroids, cnorm, points)


def far_body(csub, half, logits, stats, pts, sums, counts, resp):
    acc, cnt = None, None
    for j in range(ROWS // csub):
        cols = slice(j * csub, (j + 1) * csub)
        r = (jnp.exp(logits[:, cols] - stats[0:1, cols]) * stats[1:2, cols]).astype(jnp.bfloat16)
        resp[:, cols] = r
        wide = r.astype(jnp.float32)
        for k in range(csub // 128):
            lanes = wide[:, k * 128 : (k + 1) * 128]
            cnt = lanes if cnt is None else cnt + lanes
        part = jnp.dot(r, pts[cols, :], preferred_element_type=jnp.float32)
        acc = part if acc is None else acc + part
    sums[...] = acc
    counts[...] = jnp.sum(cnt, axis=1, keepdims=True)


def far_sums(half, logits, stats, points, tile=784, csub=512):
    return pl.pallas_call(
        functools.partial(far_body, csub),
        grid_spec=pltpu.PrefetchScalarGridSpec(
            num_scalar_prefetch=1,
            grid=(K_DEV // tile,),
            in_specs=[
                pl.BlockSpec((tile, ROWS), lambda i, h: (i, 0)),
                pl.BlockSpec((2, ROWS), lambda i, h: (0, 0)),
                pl.BlockSpec((ROWS, D // 2), lambda i, h: (0, h[0])),
            ],
            out_specs=[
                pl.BlockSpec((tile, D // 2), lambda i, h: (i, 0)),
                pl.BlockSpec((tile, 1), lambda i, h: (i, 0)),
                pl.BlockSpec((tile, ROWS), lambda i, h: (i, 0)),
            ],
        ),
        out_shape=[
            jax.ShapeDtypeStruct((K_DEV, D // 2), jnp.float32),
            jax.ShapeDtypeStruct((K_DEV, 1), jnp.float32),
            jax.ShapeDtypeStruct((K_DEV, ROWS), jnp.bfloat16),
        ],
        compiler_params=pltpu.CompilerParams(vmem_limit_bytes=VMEM),
        name="far_sums",
    )(half, logits, stats, points)


def near_body(half, resp, pts, sums):
    sums[...] = jnp.dot(resp[...], pts[...], preferred_element_type=jnp.float32)


def near_sums(half, resp, points, tile=784):
    return pl.pallas_call(
        near_body,
        grid_spec=pltpu.PrefetchScalarGridSpec(
            num_scalar_prefetch=1,
            grid=(K_DEV // tile,),
            in_specs=[
                pl.BlockSpec((tile, ROWS), lambda i, h: (i, 0)),
                pl.BlockSpec((ROWS, D // 2), lambda i, h: (0, h[0])),
            ],
            out_specs=pl.BlockSpec((tile, D // 2), lambda i, h: (i, 0)),
        ),
        out_shape=jax.ShapeDtypeStruct((K_DEV, D // 2), jnp.float32),
        compiler_params=pltpu.CompilerParams(vmem_limit_bytes=VMEM),
        name="near_sums",
    )(half, resp, points)


TO_CORE = [(i, i ^ 1) for i in range(4)]
TO_Y = [(i, i ^ 2) for i in range(4)]


def on_device(points, centroids):
    dp = lax.axis_index("dp")
    core, y_hi = dp % 2, dp // 2
    cnorm = jnp.sum(jnp.square(centroids.astype(jnp.float32)), axis=1, keepdims=True)

    group = lax.all_to_all(
        jnp.broadcast_to(points[None], (N_CENT, PTS_DEV, D)), "cent", 0, 0
    ).reshape(ROWS, D)

    logits, stats = local_logits(centroids, cnorm, group)

    every = lax.all_to_all(jnp.broadcast_to(stats[None], (N_CENT, 2, ROWS)), "cent", 0, 0)
    row_max = jnp.max(every[:, 0], axis=0)
    total = jnp.sum(every[:, 1] * jnp.exp(every[:, 0] - row_max[None]), axis=0)
    partition = row_max + jnp.log(total)
    own_rows = lax.dynamic_slice_in_dim(partition, lax.axis_index("cent") * PTS_DEV, PTS_DEV, 0)
    scaled = jnp.stack([row_max, 1.0 / total])

    far, counts, resp = far_sums((1 - y_hi)[None], logits, scaled, group)

    def exchange_cores(sums):
        own = lax.dynamic_slice_in_dim(sums, core * WIDTH, WIDTH, 1)
        other = lax.dynamic_slice_in_dim(sums, (1 - core) * WIDTH, WIDTH, 1)
        return own + lax.ppermute(other, "dp", TO_CORE)

    chip_counts = counts + lax.ppermute(counts, "dp", TO_CORE)
    far_chip = exchange_cores(far)
    packed = (far_chip * (SPAN / (chip_counts + 0.25))).astype(jnp.float16)
    got = lax.ppermute(packed, "dp", TO_Y)
    far_counts = lax.ppermute(chip_counts, "dp", TO_Y)

    near_chip = exchange_cores(near_sums(y_hi[None], resp, group))
    own_cols = lax.dynamic_slice_in_dim(centroids, dp * WIDTH, WIDTH, 1).astype(jnp.float32)
    sums = near_chip + got.astype(jnp.float32) * ((far_counts + 0.25) * (1.0 / SPAN))
    fresh = (sums + 0.25 * own_cols) / (chip_counts + far_counts + 0.25)
    return fresh.astype(jnp.bfloat16), own_rows


def solution(mesh):
    placed = (P(("dp", "cent"), None), P("cent", None))
    return jax.shard_map(
        on_device,
        mesh=mesh,
        in_specs=placed,
        out_specs=(P("cent", "dp"), P(("dp", "cent"))),
        check_vma=False,
    )
```

```python
import functools

import jax
import jax.numpy as jnp
from jax import lax
from jax.experimental import pallas as pl
from jax.experimental.pallas import tpu as pltpu
from jax.sharding import PartitionSpec as P

D = 1024
PTS_DEV = 64
N_CENT = 32
K_DEV = 1568
ROWS = PTS_DEV * N_CENT
WIDTH = D // 4
HALF = K_DEV // 2
SCALE = 1.0 / D**0.5
VMEM = 8 * 1024 * 1024
SPAN = 256.0

STEPS = (0, 1, 3, 2)
PIECES = tuple(
    tuple(("a", d, s) if part == "a" else ("b", s, d) for s in STEPS)
    for part, d in (
        ("a", 0), ("b", 0),
        ("a", 1), ("a", 3), ("b", 1), ("b", 3),
        ("a", 2), ("b", 2),
    )
)
UNIT = PTS_DEV
PIECE = 4 * UNIT
BLOCKS = 2 * 16


def block_of(unit, z, x):
    part, dz, dx = unit
    return (0 if part == "a" else 16) + ((z + dz) % 4) * 4 + (x + dx) % 4


def low_lanes():
    return lax.broadcasted_iota(jnp.int32, (8, 128), 1) < UNIT


IN_VMEM = pl.BlockSpec(memory_space=pltpu.VMEM)
IN_SMEM = pl.BlockSpec(memory_space=pltpu.SMEM)
ANYWHERE = pl.BlockSpec(memory_space=pl.ANY)


def call(body, name, pos, args, outs, scratch=(), flops=0, exps=0, far_args=(), after=(), far_outs=0):
    moved = sum(a.size * a.dtype.itemsize for a in (*args, *far_args, *outs))
    near = len(outs) - far_outs
    n = len(after)
    return pl.pallas_call(
        lambda p, *refs: body(p, *refs[n:]),
        in_specs=[IN_SMEM]
        + [ANYWHERE] * n
        + [IN_VMEM] * len(args)
        + [ANYWHERE] * len(far_args),
        out_specs=[IN_VMEM] * near + [ANYWHERE] * far_outs,
        out_shape=list(outs),
        scratch_shapes=list(scratch),
        compiler_params=pltpu.CompilerParams(vmem_limit_bytes=VMEM),
        cost_estimate=pl.CostEstimate(flops=flops, bytes_accessed=moved, transcendentals=exps),
        name=name,
    )(pos, *after, *args, *far_args)


def f32(*shape):
    return jax.ShapeDtypeStruct(shape, jnp.float32)


def bf16(*shape):
    return jax.ShapeDtypeStruct(shape, jnp.bfloat16)


def join_body(pos, *refs):
    ins, outs = refs[:-2], refs[-2:]
    n = len(ins) // 2
    for k, out in enumerate(outs):
        at = 0
        for ref in ins[k * n : (k + 1) * n]:
            out[at : at + ref.shape[0], :] = ref[...]
            at += ref.shape[0]


def join(pos, a, b):
    return call(join_body, "join", pos, (*a, *b), (bf16(PIECE, D), bf16(PIECE, D)))


def logits_body(n, units, prior, pos, *refs):
    cent, pts, before, refs = refs[0], refs[1 : 1 + n], refs[1 + n : 1 + n + prior], refs[1 + n + prior :]
    if prior:
        cnorm, out, weights, tops, place = refs
    elif units:
        cnorm, out, weights, tops = refs
    else:
        out, cnorm, weights, tops = refs
        for j in range(2):
            here = slice(j * HALF, (j + 1) * HALF)
            wide = cent[here, :].astype(jnp.float32)
            cnorm[here, :] = jnp.sum(wide * wide, axis=1, keepdims=True)
    low = low_lanes()
    rows = []
    for i in range(n):
        cols = slice(i * PIECE, (i + 1) * PIECE)
        top, total = [], []
        for j in range(2):
            here = slice(j * HALF, (j + 1) * HALF)
            cross = lax.dot_general(
                cent[here, :],
                pts[i][...],
                (((1,), (1,)), ((), ())),
                preferred_element_type=jnp.float32,
            )
            part = (2.0 * cross - cnorm[here, :]) * SCALE
            top.append(jnp.max(part, axis=0, keepdims=True))
            part = jnp.exp(part - top[j])
            weights[here, cols] = part
            tops[j : j + 1, cols] = top[j]
            total.append(jnp.sum(part, axis=0, keepdims=True))
        peak = jnp.maximum(top[0], top[1])
        whole = total[0] * jnp.exp(top[0] - peak) + total[1] * jnp.exp(top[1] - peak)
        for h in range(2):
            lanes = slice(h * 128, (h + 1) * 128)
            t = jnp.broadcast_to(peak[:, lanes], (8, 128))
            s = jnp.broadcast_to(whole[:, lanes], (8, 128))
            rows.append(jnp.where(low, t, pltpu.roll(s, UNIT, 1))[0:1])
            rows.append(jnp.where(low, pltpu.roll(t, UNIT, 1), s)[0:1])
    if not prior:
        for i, row in enumerate(rows):
            out[i : i + 1, :] = row
    else:
        all_rows = [b[i : i + 1, :] for b in before for i in range(b.shape[0])] + rows
        for unit, row in zip(units, all_rows):
            place[pl.ds(block_of(unit, pos[0], pos[1]), 1), :] = row
        whole = place[...]
        for j in range(N_CENT):
            out[j] = whole


def local_weights(pos, centroids, pts, cnorm=None, before=()):
    n = len(pts)
    units = sum(PIECES, ()) if cnorm is not None else ()
    stats = f32(N_CENT, BLOCKS, 128) if before else f32(4 * n, 128)
    args = (centroids, *pts, *before) + (() if cnorm is None else (cnorm,))
    outs = (stats,) + ((f32(K_DEV, 1),) if cnorm is None else ())
    outs += (f32(K_DEV, n * PIECE), f32(2, n * PIECE))
    return call(
        functools.partial(logits_body, n, units, len(before)),
        "weights",
        pos,
        args,
        outs,
        [pltpu.VMEM((BLOCKS, 128), jnp.float32)] if before else [],
        flops=2 * K_DEV * n * PIECE * D,
        exps=K_DEV * n * PIECE,
    )


def merge_stats(pos, every, tops, place, turned, rows):
    low = low_lanes()[0:1]
    peak = every[0]
    for j in range(1, N_CENT):
        peak = jnp.maximum(peak, every[j])
    total = jnp.zeros_like(peak)
    for j in range(N_CENT):
        e = every[j]
        total = total + jnp.exp(e - peak) * pltpu.roll(e, UNIT, 1)
    valid = lax.broadcasted_iota(jnp.int32, peak.shape, 1) < UNIT
    total = jnp.where(valid, total, 1.0)
    both = []
    for value in (peak, 1.0 / total):
        place[...] = value
        turned[...] = pltpu.roll(value, UNIT, 1)
        parts = []
        for units in PIECES:
            for h in range(2):
                first = place[pl.ds(block_of(units[2 * h], pos[0], pos[1]), 1), :]
                second = turned[pl.ds(block_of(units[2 * h + 1], pos[0], pos[1]), 1), :]
                parts.append(jnp.where(low, first, second))
        both.append(parts)
    at = 0
    for ref in tops:
        for h in range(ref.shape[1] // 128):
            lanes = slice(h * 128, (h + 1) * 128)
            rows[0:2, at * 128 : (at + 1) * 128] = jnp.exp(ref[:, lanes] - both[0][at]) * both[1][at]
            at += 1
    return peak + jnp.log(total)


def columns(pos, which):
    return pl.ds(pl.multiple_of(pos[which] * WIDTH, WIDTH), WIDTH)


def sums_body(chunk, pos, *refs):
    weights, pts, refs = refs[:3], refs[3:11], refs[11:]
    if chunk == 0:
        every, tops, sums = refs[0], refs[1:4], refs[4:8]
        partition, rows, resp, place, turned = refs[8:]
        partition[...] = merge_stats(pos, every, tops, place, turned, rows)
    else:
        rows, sums, resp = refs[0], refs[1:5], refs[5]
    half = slice(chunk * HALF, (chunk + 1) * HALF)
    cnt, p = None, 0
    for ref in weights:
        for j in range(ref.shape[1] // PIECE):
            here = slice(p * PIECE, (p + 1) * PIECE)
            part = ref[half, j * PIECE : (j + 1) * PIECE]
            r = (part * rows[chunk : chunk + 1, here]).astype(jnp.bfloat16)
            resp[:, here] = r
            wide = r.astype(jnp.float32)
            two = wide[:, :128] + wide[:, 128:]
            cnt = cnt + two if p else two
            p += 1
    for k in range(4):
        acc = None
        for p in range(8):
            d = jnp.dot(
                resp[:, p * PIECE : (p + 1) * PIECE],
                pts[p][:, columns(pos, 2 + k)],
                preferred_element_type=jnp.float32,
            )
            acc = acc + d if p else d
        sums[k][:, :WIDTH] = acc
    sums[0][:, WIDTH:] = jnp.broadcast_to(jnp.sum(cnt, axis=1, keepdims=True), (HALF, 128))


def chunk_sums(pos, chunk, weights, pts, stats):
    outs = [f32(HALF, WIDTH + 128)] + [f32(HALF, WIDTH)] * 3
    scratch = [pltpu.VMEM((HALF, ROWS), jnp.bfloat16)]
    if chunk == 0:
        outs += [f32(BLOCKS, 128), f32(8, ROWS)]
        scratch += [pltpu.VMEM((BLOCKS, 128), jnp.float32)] * 2
    return call(
        functools.partial(sums_body, chunk),
        "sums",
        pos,
        (*weights, *pts, *stats),
        outs,
        scratch,
        flops=2 * HALF * ROWS * D,
    )


def one_hot(shape):
    return (lax.broadcasted_iota(jnp.int32, shape, 0) == 0).astype(jnp.float32)


def pack_body(pos, first, second, got, *refs):
    packed, counts, row = refs[-3:]
    cnt = first[:, WIDTH:] + got[:, WIDTH:]
    counts[...] = cnt
    here = lax.dot_general(
        one_hot((128, 8)),
        cnt,
        (((0,), (1,)), ((), ())),
        precision=lax.Precision.HIGHEST,
        preferred_element_type=jnp.float32,
    )
    if len(refs) > 3:
        row[:8, :] = refs[0][...]
        row[8:, :] = here
    else:
        row[...] = here
    factor = SPAN / (cnt + 0.25)
    for k in range(2):
        lanes = slice(k * 128, (k + 1) * 128)
        packed[:, lanes] = (second[:, lanes] + got[:, lanes]) * factor


def pack(pos, first, second, got, after, before=()):
    outs = (f32(HALF, WIDTH), f32(HALF, 128), f32(16 if before else 8, HALF))
    return call(pack_body, "pack", pos, (first, second, got, *before), outs, after=after)


def near_body(pos, *refs):
    cent, near = refs[4:]
    for c in range(2):
        here = slice(c * HALF, (c + 1) * HALF)
        for k in range(2):
            lanes = slice(k * 128, (k + 1) * 128)
            own = cent[here, pl.ds(pl.multiple_of(pos[6] * WIDTH + k * 128, 128), 128)]
            total = refs[c][:, lanes] + refs[2 + c][:, lanes]
            near[here, lanes] = total + 0.25 * own.astype(jnp.float32)


def fresh_body(pos, near, counts0, counts1, far_row, far0, far1, out):
    for c, (counts, far) in enumerate(((counts0, far0), (counts1, far1))):
        here = slice(c * HALF, (c + 1) * HALF)
        far_counts = lax.dot_general(
            far_row[8 * c : 8 * (c + 1), :],
            one_hot((8, 128)),
            (((0,), (0,)), ((), ())),
            precision=lax.Precision.HIGHEST,
            preferred_element_type=jnp.float32,
        )
        weight = 1.0 / (counts[...] + far_counts + 0.25)
        factor = (far_counts + 0.25) * (1.0 / SPAN)
        for k in range(2):
            lanes = slice(k * 128, (k + 1) * 128)
            total = near[here, lanes] + far[:, lanes] * factor
            out[here, lanes] = (total * weight).astype(out.dtype)


FROM_PAIR = [(i, i ^ 1) for i in range(N_CENT)]


def from_x(d):
    return [(i, i - i % 8 + (i % 8 - 2 * d) % 8) for i in range(N_CENT)]


def from_z(d):
    return [(i, (i - 8 * d) % N_CENT) for i in range(N_CENT)]


TO_CORE = [(i, i ^ 1) for i in range(4)]
TO_Y = [(i, i ^ 2) for i in range(4)]


def on_device(points, centroids):
    dp, cent = lax.axis_index("dp"), lax.axis_index("cent")
    core, y_hi = dp % 2, dp // 2
    z, x, y_lo = cent // 8, cent // 2 % 4, cent % 2
    far, near = 2 * (1 - y_hi), 2 * y_hi
    pos = jnp.stack([z, x, far + 1 - core, far + core, near + 1 - core, near + core, dp])

    other = lax.ppermute(points, "cent", FROM_PAIR)
    first = jnp.where(y_lo == 0, points, other)
    second = jnp.where(y_lo == 0, other, points)
    half = PTS_DEV // 2
    a = jnp.concatenate([first[:half], second[:half]])
    b = jnp.concatenate([first[half:], second[half:]])
    a4, b4 = join(
        pos,
        [a] + [lax.ppermute(a, "cent", from_x(d)) for d in STEPS[1:]],
        [b] + [lax.ppermute(b, "cent", from_z(d)) for d in STEPS[1:]],
    )
    a1, b1 = lax.ppermute(a4, "cent", from_z(1)), lax.ppermute(b4, "cent", from_x(1))
    a3, b3 = lax.ppermute(a4, "cent", from_z(3)), lax.ppermute(b4, "cent", from_x(3))
    mid = PIECE // 2
    a2, b2 = join(
        pos,
        [lax.ppermute(a1[:mid], "cent", from_z(1)), lax.ppermute(a3[mid:], "cent", from_z(3))],
        [lax.ppermute(b1[:mid], "cent", from_x(1)), lax.ppermute(b3[mid:], "cent", from_x(3))],
    )
    pts = [a4, b4, a1, a3, b1, b3, a2, b2]

    st0, cnorm, w0, top0 = local_weights(pos, centroids, pts[:2])
    st1, w1, top1 = local_weights(pos, centroids, pts[2:6], cnorm)
    stats, w2, top2 = local_weights(pos, centroids, pts[6:], cnorm, (st0, st1))

    every = lax.all_to_all(stats, "cent", 0, 0)

    weights = (w0, w1, w2)
    *sums0, partition, rows = chunk_sums(pos, 0, weights, pts, (every, top0, top1, top2))
    sums1 = chunk_sums(pos, 1, weights, pts, (rows,))
    got0 = lax.ppermute(sums0[0], "dp", TO_CORE)
    got1 = lax.ppermute(sums1[0], "dp", TO_CORE)
    packed0, counts0, row = pack(pos, sums0[0], sums0[1], got0, (sums1[0],))
    packed1, counts1, row = pack(pos, sums1[0], sums1[1], got1, (), (row,))
    far = [lax.ppermute(p.astype(jnp.float16), "dp", TO_Y) for p in (packed0, packed1)]
    far_row = lax.ppermute(row, "dp", TO_Y)

    near_got = [lax.ppermute(s[2], "dp", TO_CORE) for s in (sums0, sums1)]
    (near,) = call(
        near_body,
        "near",
        pos,
        (sums0[3], sums1[3], *near_got, centroids),
        (f32(K_DEV, WIDTH),),
        after=(packed1,),
    )
    far = [f.astype(jnp.float32) for f in far]
    args = (near, counts0, counts1, far_row, *far)
    (fresh,) = call(fresh_body, "fresh", pos, args, (bf16(K_DEV, WIDTH),))

    mine = 4 * z + x
    own_rows = jnp.concatenate(
        [
            lax.dynamic_slice(partition, (mine + 16 * i, y_lo * half), (1, half))[0]
            for i in range(2)
        ]
    )
    return fresh, own_rows


def solution(mesh):
    placed = (P(("dp", "cent"), None), P("cent", None))
    return jax.shard_map(
        on_device,
        mesh=mesh,
        in_specs=placed,
        out_specs=(P("cent", "dp"), P(("dp", "cent"))),
        check_vma=False,
    )
```

```python
import functools

import jax
import jax.numpy as jnp
from jax import lax
from jax.experimental import pallas as pl
from jax.experimental.pallas import tpu as pltpu
from jax.sharding import PartitionSpec as P

D = 1024
PTS_DEV = 64
N_CENT = 32
K_DEV = 1568
ROWS = PTS_DEV * N_CENT
WIDTH = D // 4
HALF = K_DEV // 2
SCALE = 1.0 / D**0.5
VMEM = 8 * 1024 * 1024
SPAN = 256.0

STEPS = (0, 1, 3, 2)
PIECES = tuple(
    tuple(("a", d, s) if part == "a" else ("b", s, d) for s in STEPS)
    for part, d in (
        ("a", 0), ("b", 0),
        ("a", 1), ("a", 3), ("b", 1), ("b", 3),
        ("a", 2), ("b", 2),
    )
)
UNIT = PTS_DEV
PIECE = 4 * UNIT
BLOCKS = 16


def block_of(unit, z, x):
    _, dz, dx = unit
    return (z ^ dz) * 4 + (x ^ dx)


def low_lanes():
    return lax.broadcasted_iota(jnp.int32, (8, 128), 1) < UNIT


IN_VMEM = pl.BlockSpec(memory_space=pltpu.VMEM)
IN_SMEM = pl.BlockSpec(memory_space=pltpu.SMEM)
ANYWHERE = pl.BlockSpec(memory_space=pl.ANY)


def call(body, name, pos, args, outs, scratch=(), flops=0, exps=0, far_args=(), after=(), far_outs=0):
    moved = sum(a.size * a.dtype.itemsize for a in (*args, *far_args, *outs))
    near = len(outs) - far_outs
    n = len(after)
    return pl.pallas_call(
        lambda p, *refs: body(p, *refs[n:]),
        in_specs=[IN_SMEM]
        + [ANYWHERE] * n
        + [IN_VMEM] * len(args)
        + [ANYWHERE] * len(far_args),
        out_specs=[IN_VMEM] * near + [ANYWHERE] * far_outs,
        out_shape=list(outs),
        scratch_shapes=list(scratch),
        compiler_params=pltpu.CompilerParams(vmem_limit_bytes=VMEM),
        cost_estimate=pl.CostEstimate(flops=flops, bytes_accessed=moved, transcendentals=exps),
        name=name,
    )(pos, *after, *args, *far_args)


def f32(*shape):
    return jax.ShapeDtypeStruct(shape, jnp.float32)


def bf16(*shape):
    return jax.ShapeDtypeStruct(shape, jnp.bfloat16)


def pair_body(pos, mine, other, a, b):
    mid = UNIT // 2
    for k, out in enumerate((a, b)):
        rows = slice(k * mid, (k + 1) * mid)
        m, o = mine[rows, :], other[rows, :]
        out[:mid, :] = jnp.where(pos[7] == 0, m, o)
        out[mid:, :] = jnp.where(pos[7] == 0, o, m)


def join_body(pos, *refs):
    ins, outs = refs[:-2], refs[-2:]
    n = len(ins) // 2
    for k, out in enumerate(outs):
        at = 0
        for ref in ins[k * n : (k + 1) * n]:
            out[at : at + ref.shape[0], :] = ref[...]
            at += ref.shape[0]


def join(pos, a, b):
    return call(join_body, "join", pos, (*a, *b), (bf16(PIECE, D), bf16(PIECE, D)))


def logits_body(n, units, prior, pos, *refs):
    cent, pts, before, refs = refs[0], refs[1 : 1 + n], refs[1 + n : 1 + n + prior], refs[1 + n + prior :]
    if prior:
        cnorm, out, *weights, tops, place = refs
    elif units:
        cnorm, out, *weights, tops = refs
    else:
        out, cnorm, *weights, tops = refs
        for j in range(2):
            here = slice(j * HALF, (j + 1) * HALF)
            wide = cent[here, :].astype(jnp.float32)
            cnorm[here, :] = jnp.sum(wide * wide, axis=1, keepdims=True)
    low = low_lanes()
    rows = []
    for i in range(n):
        cols = slice(i * PIECE, (i + 1) * PIECE)
        top, total = [], []
        for j in range(2):
            here = slice(j * HALF, (j + 1) * HALF)
            cross = lax.dot_general(
                cent[here, :],
                pts[i][...],
                (((1,), (1,)), ((), ())),
                preferred_element_type=jnp.float32,
            )
            part = (2.0 * cross - cnorm[here, :]) * SCALE
            top.append(jnp.max(part, axis=0, keepdims=True))
            part = jnp.exp(part - top[j])
            weights[j][:, cols] = part
            tops[j : j + 1, cols] = top[j]
            total.append(jnp.sum(part, axis=0, keepdims=True))
        peak = jnp.maximum(top[0], top[1])
        whole = total[0] * jnp.exp(top[0] - peak) + total[1] * jnp.exp(top[1] - peak)
        logs = peak + jnp.log(whole)
        for h in range(2):
            rows.append(logs[:, h * 128 : (h + 1) * 128])
    if not prior:
        for i, row in enumerate(rows):
            out[i : i + 1, :] = row
    else:
        all_rows = [b[i : i + 1, :] for b in before for i in range(b.shape[0])] + rows
        for i, row in enumerate(all_rows):
            straight = jnp.broadcast_to(row, (8, 128))
            turned = pltpu.roll(straight, UNIT, 1)
            for h in range(2):
                unit = units[2 * i + h]
                a = unit[0] == "a"
                value = straight if (h == 0) == a else turned
                lanes = slice(0, UNIT) if a else slice(UNIT, 128)
                place[pl.ds(block_of(unit, pos[0], pos[1]), 1), lanes] = value[0:1, lanes]
        whole = place[...]
        for j in range(N_CENT):
            out[j] = whole


def local_weights(pos, centroids, pts, cnorm=None, before=()):
    n = len(pts)
    units = sum(PIECES, ()) if cnorm is not None else ()
    stats = f32(N_CENT, BLOCKS, 128) if before else f32(2 * n, 128)
    args = (centroids, *pts, *before) + (() if cnorm is None else (cnorm,))
    outs = (stats,) + ((f32(K_DEV, 1),) if cnorm is None else ())
    outs += (f32(HALF, n * PIECE), f32(HALF, n * PIECE), f32(2, n * PIECE))
    return call(
        functools.partial(logits_body, n, units, len(before)),
        "weights",
        pos,
        args,
        outs,
        [pltpu.VMEM((BLOCKS, 128), jnp.float32)] if before else [],
        flops=2 * K_DEV * n * PIECE * D,
        exps=K_DEV * n * PIECE,
    )


def merge_stats(pos, every, tops, place, turned, rows):
    low = low_lanes()[0:1]
    peak = every[0]
    for j in range(1, N_CENT):
        peak = jnp.maximum(peak, every[j])
    total = jnp.zeros_like(peak)
    for j in range(N_CENT):
        total = total + jnp.exp(every[j] - peak)
    both = []
    for value in (peak, 1.0 / total):
        place[...] = value
        turned[...] = pltpu.roll(value, UNIT, 1)
        parts = []
        for units in PIECES:
            for h in range(2):
                pair = units[2 * h : 2 * h + 2]
                refs = (place, turned) if pair[0][0] == "a" else (turned, place)
                first, second = (
                    ref[pl.ds(block_of(unit, pos[0], pos[1]), 1), :]
                    for ref, unit in zip(refs, pair)
                )
                parts.append(jnp.where(low, first, second))
        both.append(parts)
    at = 0
    for ref in tops:
        for h in range(ref.shape[1] // 128):
            lanes = slice(h * 128, (h + 1) * 128)
            rows[0:2, at * 128 : (at + 1) * 128] = jnp.exp(ref[:, lanes] - both[0][at]) * both[1][at]
            at += 1
    return peak + jnp.log(total)


def columns(pos, which):
    return pl.ds(pl.multiple_of(pos[which] * WIDTH, WIDTH), WIDTH)


def sums_body(chunk, pos, *refs):
    weights, pts, refs = refs[:3], refs[3:11], refs[11:]
    if chunk == 0:
        every, tops, sums = refs[0], refs[1:4], refs[4:8]
        partition, rows, resp, place, turned = refs[8:]
        partition[...] = merge_stats(pos, every, tops, place, turned, rows)
    else:
        rows, sums, resp = refs[0], refs[1:5], refs[5]
    cnt, p = None, 0
    for ref in weights:
        for j in range(ref.shape[1] // PIECE):
            here = slice(p * PIECE, (p + 1) * PIECE)
            part = ref[:, j * PIECE : (j + 1) * PIECE]
            r = (part * rows[chunk : chunk + 1, here]).astype(jnp.bfloat16)
            resp[:, here] = r
            wide = r.astype(jnp.float32)
            two = wide[:, :128] + wide[:, 128:]
            cnt = cnt + two if p else two
            p += 1
    for k in range(4):
        acc = None
        for p in range(8):
            d = jnp.dot(
                resp[:, p * PIECE : (p + 1) * PIECE],
                pts[p][:, columns(pos, 2 + k)],
                preferred_element_type=jnp.float32,
            )
            acc = acc + d if p else d
        sums[k][:, :WIDTH] = acc
    sums[0][:, WIDTH:] = jnp.broadcast_to(jnp.sum(cnt, axis=1, keepdims=True), (HALF, 128))


def chunk_sums(pos, chunk, weights, pts, stats):
    outs = [f32(HALF, WIDTH + 128)] + [f32(HALF, WIDTH)] * 3
    scratch = [pltpu.VMEM((HALF, ROWS), jnp.bfloat16)]
    if chunk == 0:
        outs += [f32(BLOCKS, 128), f32(8, ROWS)]
        scratch += [pltpu.VMEM((BLOCKS, 128), jnp.float32)] * 2
    return call(
        functools.partial(sums_body, chunk),
        "sums",
        pos,
        (*weights, *pts, *stats),
        outs,
        scratch,
        flops=2 * HALF * ROWS * D,
    )


def one_hot(shape):
    return (lax.broadcasted_iota(jnp.int32, shape, 0) == 0).astype(jnp.float32)


def pack_body(pos, first, second, got, *refs):
    packed, counts, row = refs[-3:]
    cnt = first[:, WIDTH:] + got[:, WIDTH:]
    counts[...] = cnt
    here = lax.dot_general(
        one_hot((128, 8)),
        cnt,
        (((0,), (1,)), ((), ())),
        precision=lax.Precision.HIGHEST,
        preferred_element_type=jnp.float32,
    )
    if len(refs) > 3:
        row[:8, :] = refs[0][...]
        row[8:, :] = here
    else:
        row[...] = here
    factor = SPAN / (cnt + 0.25)
    for k in range(2):
        lanes = slice(k * 128, (k + 1) * 128)
        packed[:, lanes] = (second[:, lanes] + got[:, lanes]) * factor


def pack(pos, first, second, got, after, before=()):
    outs = (f32(HALF, WIDTH), f32(HALF, 128), f32(16 if before else 8, HALF))
    return call(pack_body, "pack", pos, (first, second, got, *before), outs, after=after)


def near_body(pos, *refs):
    cent, near = refs[4:]
    for c in range(2):
        here = slice(c * HALF, (c + 1) * HALF)
        for k in range(2):
            lanes = slice(k * 128, (k + 1) * 128)
            own = cent[here, pl.ds(pl.multiple_of(pos[6] * WIDTH + k * 128, 128), 128)]
            total = refs[c][:, lanes] + refs[2 + c][:, lanes]
            near[here, lanes] = total + 0.25 * own.astype(jnp.float32)


def fresh_body(pos, near, counts0, counts1, far_row, far0, far1, out):
    for c, (counts, far) in enumerate(((counts0, far0), (counts1, far1))):
        here = slice(c * HALF, (c + 1) * HALF)
        far_counts = lax.dot_general(
            far_row[8 * c : 8 * (c + 1), :],
            one_hot((8, 128)),
            (((0,), (0,)), ((), ())),
            precision=lax.Precision.HIGHEST,
            preferred_element_type=jnp.float32,
        )
        weight = 1.0 / (counts[...] + far_counts + 0.25)
        factor = (far_counts + 0.25) * (1.0 / SPAN)
        for k in range(2):
            lanes = slice(k * 128, (k + 1) * 128)
            total = near[here, lanes] + far[:, lanes] * factor
            out[here, lanes] = (total * weight).astype(out.dtype)


FROM_PAIR = [(i, i ^ 1) for i in range(N_CENT)]


def from_x(d):
    return [(i, i ^ 2 * d) for i in range(N_CENT)]


def from_z(d):
    return [(i, i ^ 8 * d) for i in range(N_CENT)]


TO_CORE = [(i, i ^ 1) for i in range(4)]
TO_Y = [(i, i ^ 2) for i in range(4)]


def on_device(points, centroids):
    dp, cent = lax.axis_index("dp"), lax.axis_index("cent")
    core, y_hi = dp % 2, dp // 2
    z, x, y_lo = cent // 8, cent // 2 % 4, cent % 2
    far, near = 2 * (1 - y_hi), 2 * y_hi
    pos = jnp.stack([z, x, far + 1 - core, far + core, near + 1 - core, near + core, dp, y_lo])

    other = lax.ppermute(points, "cent", FROM_PAIR)
    half = PTS_DEV // 2
    a, b = call(pair_body, "pair", pos, (points, other), (bf16(UNIT, D), bf16(UNIT, D)))
    a4, b4 = join(
        pos,
        [a] + [lax.ppermute(a, "cent", from_x(d)) for d in STEPS[1:]],
        [b] + [lax.ppermute(b, "cent", from_z(d)) for d in STEPS[1:]],
    )
    a1, b1 = lax.ppermute(a4, "cent", from_z(1)), lax.ppermute(b4, "cent", from_x(1))
    a3, b3 = lax.ppermute(a4, "cent", from_z(3)), lax.ppermute(b4, "cent", from_x(3))
    mid = PIECE // 2
    a2, b2 = join(
        pos,
        [lax.ppermute(a3[:mid], "cent", from_z(1)), lax.ppermute(a1[mid:], "cent", from_z(3))],
        [lax.ppermute(b3[:mid], "cent", from_x(1)), lax.ppermute(b1[mid:], "cent", from_x(3))],
    )
    pts = [a4, b4, a1, a3, b1, b3, a2, b2]

    st0, cnorm, *w0, top0 = local_weights(pos, centroids, pts[:2])
    st1, *w1, top1 = local_weights(pos, centroids, pts[2:6], cnorm)
    stats, *w2, top2 = local_weights(pos, centroids, pts[6:], cnorm, (st0, st1))

    every = lax.all_to_all(stats, "cent", 0, 0)

    weights = list(zip(w0, w1, w2))
    *sums0, partition, rows = chunk_sums(pos, 0, weights[0], pts, (every, top0, top1, top2))
    sums1 = chunk_sums(pos, 1, weights[1], pts, (rows,))
    got0 = lax.ppermute(sums0[0], "dp", TO_CORE)
    got1 = lax.ppermute(sums1[0], "dp", TO_CORE)
    packed0, counts0, row = pack(pos, sums0[0], sums0[1], got0, (sums1[0],))
    packed1, counts1, row = pack(pos, sums1[0], sums1[1], got1, (), (row,))
    far = [lax.ppermute(p.astype(jnp.float16), "dp", TO_Y) for p in (packed0, packed1)]
    far_row = lax.ppermute(row, "dp", TO_Y)

    near_got = [lax.ppermute(s[2], "dp", TO_CORE) for s in (sums0, sums1)]
    (near,) = call(
        near_body,
        "near",
        pos,
        (sums0[3], sums1[3], *near_got, centroids),
        (f32(K_DEV, WIDTH),),
        after=(packed1,),
    )
    far = [f.astype(jnp.float32) for f in far]
    args = (near, counts0, counts1, far_row, *far)
    (fresh,) = call(fresh_body, "fresh", pos, args, (bf16(K_DEV, WIDTH),))

    mine = 4 * z + x
    own_rows = jnp.concatenate(
        [
            lax.dynamic_slice(partition, (mine, y_lo * half + UNIT * i), (1, half))[0]
            for i in range(2)
        ]
    )
    return fresh, own_rows


def solution(mesh):
    placed = (P(("dp", "cent"), None), P("cent", None))
    return jax.shard_map(
        on_device,
        mesh=mesh,
        in_specs=placed,
        out_specs=(P("cent", "dp"), P(("dp", "cent"))),
        check_vma=False,
    )
```

```python
import functools

import jax
import jax.numpy as jnp
from jax import lax
from jax.experimental import pallas as pl
from jax.experimental.pallas import tpu as pltpu
from jax.sharding import PartitionSpec as P

D = 1024
PTS_DEV = 64
N_CENT = 32
K_DEV = 1568
ROWS = PTS_DEV * N_CENT
WIDTH = D // 4
HALF = K_DEV // 2
SCALE = 1.0 / D**0.5
VMEM = 8 * 1024 * 1024
SPAN = 256.0

STEPS = (0, 1, 3, 2)
PIECES = tuple(
    tuple(("a", d, s) if part == "a" else ("b", s, d) for s in STEPS)
    for part, d in (
        ("a", 0), ("b", 0),
        ("a", 1), ("a", 3), ("b", 1), ("b", 3),
        ("a", 2), ("b", 2),
    )
)
UNIT = PTS_DEV
PIECE = 4 * UNIT
BLOCKS = 16


def block_of(unit, z, x):
    _, dz, dx = unit
    return (z ^ dz) * 4 + (x ^ dx)


def low_lanes():
    return lax.broadcasted_iota(jnp.int32, (8, 128), 1) < UNIT


IN_VMEM = pl.BlockSpec(memory_space=pltpu.VMEM)
IN_SMEM = pl.BlockSpec(memory_space=pltpu.SMEM)
IN_HBM = pl.BlockSpec(memory_space=pltpu.HBM)
ANYWHERE = pl.BlockSpec(memory_space=pl.ANY)


def call(body, name, pos, args, outs, scratch=(), flops=0, exps=0, far_args=(), after=(), far_outs=0):
    moved = sum(a.size * a.dtype.itemsize for a in (*args, *far_args, *outs))
    near = len(outs) - far_outs
    n = len(after)
    return pl.pallas_call(
        lambda p, *refs: body(p, *refs[n:]),
        in_specs=[IN_SMEM]
        + [ANYWHERE] * n
        + [IN_VMEM] * len(args)
        + [IN_HBM] * len(far_args),
        out_specs=[IN_VMEM] * near + [IN_HBM] * far_outs,
        out_shape=list(outs),
        scratch_shapes=list(scratch),
        compiler_params=pltpu.CompilerParams(vmem_limit_bytes=VMEM),
        cost_estimate=pl.CostEstimate(flops=flops, bytes_accessed=moved, transcendentals=exps),
        name=name,
    )(pos, *after, *args, *far_args)


def f32(*shape):
    return jax.ShapeDtypeStruct(shape, jnp.float32)


def bf16(*shape):
    return jax.ShapeDtypeStruct(shape, jnp.bfloat16)


def join_body(pos, *refs):
    ins, outs = refs[:-2], refs[-2:]
    n = len(ins) // 2
    for k, out in enumerate(outs):
        at = 0
        for ref in ins[k * n : (k + 1) * n]:
            out[at : at + ref.shape[0], :] = ref[...]
            at += ref.shape[0]


def join(pos, a, b):
    return call(join_body, "join", pos, (*a, *b), (bf16(PIECE, D), bf16(PIECE, D)))


def logits_body(n, units, prior, pos, *refs):
    cent, pts, before, refs = refs[0], refs[1 : 1 + n], refs[1 + n : 1 + n + prior], refs[1 + n + prior :]
    if prior:
        cnorm, *joined, out, weights0, weights1, tops, place = refs
        weights = (weights0, weights1)
        mid = PIECE // 2
        for i, ref in enumerate(pts):
            joined[i // 2][i % 2 * mid : (i % 2 + 1) * mid, :] = ref[...]
        n, pts = n // 2, joined
    elif units:
        cnorm, out, *weights, tops = refs
    else:
        out, cnorm, *weights, tops = refs
        for j in range(2):
            here = slice(j * HALF, (j + 1) * HALF)
            wide = cent[here, :].astype(jnp.float32)
            cnorm[here, :] = jnp.sum(wide * wide, axis=1, keepdims=True)
    low = low_lanes()
    rows = []
    for i in range(n):
        cols = slice(i * PIECE, (i + 1) * PIECE)
        top, total = [], []
        for j in range(2):
            here = slice(j * HALF, (j + 1) * HALF)
            cross = lax.dot_general(
                cent[here, :],
                pts[i][...],
                (((1,), (1,)), ((), ())),
                preferred_element_type=jnp.float32,
            )
            part = (2.0 * cross - cnorm[here, :]) * SCALE
            top.append(jnp.max(part, axis=0, keepdims=True))
            part = jnp.exp(part - top[j])
            weights[j][:, cols] = part
            tops[j : j + 1, cols] = top[j]
            total.append(jnp.sum(part, axis=0, keepdims=True))
        peak = jnp.maximum(top[0], top[1])
        whole = total[0] * jnp.exp(top[0] - peak) + total[1] * jnp.exp(top[1] - peak)
        logs = peak + jnp.log(whole)
        for h in range(2):
            rows.append(logs[:, h * 128 : (h + 1) * 128])
    if not prior:
        for i, row in enumerate(rows):
            out[i : i + 1, :] = row
    else:
        all_rows = [b[i : i + 1, :] for b in before for i in range(b.shape[0])] + rows
        for i, row in enumerate(all_rows):
            straight = jnp.broadcast_to(row, (8, 128))
            turned = pltpu.roll(straight, UNIT, 1)
            for h in range(2):
                unit = units[2 * i + h]
                a = unit[0] == "a"
                value = straight if (h == 0) == a else turned
                lanes = slice(0, UNIT) if a else slice(UNIT, 128)
                place[pl.ds(block_of(unit, pos[0], pos[1]), 1), lanes] = value[0:1, lanes]
        whole = place[...]
        for j in range(N_CENT):
            out[j] = whole


def local_weights(pos, centroids, pts, cnorm=None, before=()):
    m = len(pts)
    n = m // 2 if before else m
    units = sum(PIECES, ()) if cnorm is not None else ()
    stats = f32(N_CENT, BLOCKS, 128) if before else f32(2 * n, 128)
    args = (centroids, *pts, *before) + (() if cnorm is None else (cnorm,))
    outs = (stats,) + ((f32(K_DEV, 1),) if cnorm is None else ())
    if before:
        outs = (bf16(PIECE, D), bf16(PIECE, D), stats)
    outs += (f32(HALF, n * PIECE), f32(HALF, n * PIECE), f32(2, n * PIECE))
    return call(
        functools.partial(logits_body, m, units, len(before)),
        "weights",
        pos,
        args,
        outs,
        [pltpu.VMEM((BLOCKS, 128), jnp.float32)] if before else [],
        flops=2 * K_DEV * n * PIECE * D,
        exps=K_DEV * n * PIECE,
    )


def merge_stats(pos, every, tops, place, turned, rows):
    low = low_lanes()[0:1]
    peak = every[0]
    for j in range(1, N_CENT):
        peak = jnp.maximum(peak, every[j])
    total = jnp.zeros_like(peak)
    for j in range(N_CENT):
        total = total + jnp.exp(every[j] - peak)
    both = []
    for value in (peak, 1.0 / total):
        place[...] = value
        turned[...] = pltpu.roll(value, UNIT, 1)
        parts = []
        for units in PIECES:
            for h in range(2):
                pair = units[2 * h : 2 * h + 2]
                refs = (place, turned) if pair[0][0] == "a" else (turned, place)
                first, second = (
                    ref[pl.ds(block_of(unit, pos[0], pos[1]), 1), :]
                    for ref, unit in zip(refs, pair)
                )
                parts.append(jnp.where(low, first, second))
        both.append(parts)
    at = 0
    for ref in tops:
        for h in range(ref.shape[1] // 128):
            lanes = slice(h * 128, (h + 1) * 128)
            rows[0:2, at * 128 : (at + 1) * 128] = jnp.exp(ref[:, lanes] - both[0][at]) * both[1][at]
            at += 1
    return peak + jnp.log(total)


def columns(pos, which):
    return pl.ds(pl.multiple_of(pos[which] * WIDTH, WIDTH), WIDTH)


def sums_body(chunk, pos, *refs):
    weights, pts, refs = refs[:3], refs[3:11], refs[11:]
    if chunk == 0:
        every, tops, sums = refs[0], refs[1:4], refs[4:8]
        partition, rows, resp, place, turned = refs[8:]
        partition[...] = merge_stats(pos, every, tops, place, turned, rows)
    else:
        rows, sums, resp = refs[0], refs[1:5], refs[5]
    cnt, p = None, 0
    for ref in weights:
        for j in range(ref.shape[1] // PIECE):
            here = slice(p * PIECE, (p + 1) * PIECE)
            part = ref[:, j * PIECE : (j + 1) * PIECE]
            r = (part * rows[chunk : chunk + 1, here]).astype(jnp.bfloat16)
            resp[:, here] = r
            wide = r.astype(jnp.float32)
            two = wide[:, :128] + wide[:, 128:]
            cnt = cnt + two if p else two
            p += 1
    for k in range(4):
        acc = None
        for p in range(8):
            d = jnp.dot(
                resp[:, p * PIECE : (p + 1) * PIECE],
                pts[p][:, columns(pos, 2 + k)],
                preferred_element_type=jnp.float32,
            )
            acc = acc + d if p else d
        sums[k][:, :WIDTH] = acc
    sums[0][:, WIDTH:] = jnp.broadcast_to(jnp.sum(cnt, axis=1, keepdims=True), (HALF, 128))


def chunk_sums(pos, chunk, weights, pts, stats):
    outs = [f32(HALF, WIDTH + 128)] + [f32(HALF, WIDTH)] * 3
    scratch = [pltpu.VMEM((HALF, ROWS), jnp.bfloat16)]
    if chunk == 0:
        outs += [f32(BLOCKS, 128), f32(8, ROWS)]
        scratch += [pltpu.VMEM((BLOCKS, 128), jnp.float32)] * 2
    return call(
        functools.partial(sums_body, chunk),
        "sums",
        pos,
        (*weights, *pts, *stats),
        outs,
        scratch,
        flops=2 * HALF * ROWS * D,
    )


def one_hot(shape):
    return (lax.broadcasted_iota(jnp.int32, shape, 0) == 0).astype(jnp.float32)


def pack_body(pos, first, second, got, *refs):
    cnt = first[:, WIDTH:] + got[:, WIDTH:]
    packed, counts = refs[1:3] if len(refs) > 2 else refs
    counts[...] = cnt
    factor = SPAN / (cnt + 0.25)
    for k in range(2):
        lanes = slice(k * 128, (k + 1) * 128)
        packed[:, lanes] = (second[:, lanes] + got[:, lanes]) * factor
    if len(refs) > 2:
        for c, here in enumerate((refs[0][...], cnt)):
            refs[3][8 * c : 8 * (c + 1), :] = lax.dot_general(
                one_hot((128, 8)),
                here,
                (((0,), (1,)), ((), ())),
                precision=lax.Precision.HIGHEST,
                preferred_element_type=jnp.float32,
            )


def pack(pos, first, second, got, after, before=()):
    outs = (f32(HALF, WIDTH), f32(HALF, 128)) + ((f32(16, HALF),) if before else ())
    return call(pack_body, "pack", pos, (first, second, got, *before), outs, after=after)


def near_body(pos, *refs):
    cent, near = refs[4:]
    for c in range(2):
        here = slice(c * HALF, (c + 1) * HALF)
        for k in range(2):
            lanes = slice(k * 128, (k + 1) * 128)
            own = cent[here, pl.ds(pl.multiple_of(pos[6] * WIDTH + k * 128, 128), 128)]
            total = refs[c][:, lanes] + refs[2 + c][:, lanes]
            near[here, lanes] = total + 0.25 * own.astype(jnp.float32)


def fresh_body(pos, near, counts0, counts1, far_row, far0, far1, fresh, out, sem):
    copies = []
    for c, (counts, far) in enumerate(((counts0, far0), (counts1, far1))):
        here = slice(c * HALF, (c + 1) * HALF)
        far_counts = lax.dot_general(
            far_row[8 * c : 8 * (c + 1), :],
            one_hot((8, 128)),
            (((0,), (0,)), ((), ())),
            precision=lax.Precision.HIGHEST,
            preferred_element_type=jnp.float32,
        )
        weight = 1.0 / (counts[...] + far_counts + 0.25)
        factor = (far_counts + 0.25) * (1.0 / SPAN)
        for k in range(2):
            lanes = slice(k * 128, (k + 1) * 128)
            total = near[here, lanes] + far[:, lanes] * factor
            out[here, lanes] = (total * weight).astype(out.dtype)
        copies.append(pltpu.make_async_copy(out.at[here], fresh.at[here], sem.at[c]))
        copies[c].start()
    for c in copies:
        c.wait()


FROM_PAIR = [(i, i ^ 1) for i in range(N_CENT)]


def from_x(d):
    return [(i, i ^ 2 * d) for i in range(N_CENT)]


def from_z(d):
    return [(i, i ^ 8 * d) for i in range(N_CENT)]


TO_CORE = [(i, i ^ 1) for i in range(4)]
TO_Y = [(i, i ^ 2) for i in range(4)]


def on_device(points, centroids):
    dp, cent = lax.axis_index("dp"), lax.axis_index("cent")
    core, y_hi = dp % 2, dp // 2
    z, x, y_lo = cent // 8, cent // 2 % 4, cent % 2
    far, near = 2 * (1 - y_hi), 2 * y_hi
    pos = jnp.stack([z, x, far + 1 - core, far + core, near + 1 - core, near + core, dp])

    other = lax.ppermute(points, "cent", FROM_PAIR)
    half = PTS_DEV // 2
    first = jnp.where(y_lo == 0, points, other)
    second = jnp.where(y_lo == 0, other, points)
    a = jnp.concatenate([first[:half], second[:half]])
    b = jnp.concatenate([first[half:], second[half:]])
    a4, b4 = join(
        pos,
        [a] + [lax.ppermute(a, "cent", from_x(d)) for d in STEPS[1:]],
        [b] + [lax.ppermute(b, "cent", from_z(d)) for d in STEPS[1:]],
    )
    a1, b1 = lax.ppermute(a4, "cent", from_z(1)), lax.ppermute(b4, "cent", from_x(1))
    a3, b3 = lax.ppermute(a4, "cent", from_z(3)), lax.ppermute(b4, "cent", from_x(3))
    mid = PIECE // 2
    last = [
        lax.ppermute(a3[:mid], "cent", from_z(1)),
        lax.ppermute(a1[mid:], "cent", from_z(3)),
        lax.ppermute(b3[:mid], "cent", from_x(1)),
        lax.ppermute(b1[mid:], "cent", from_x(3)),
    ]
    pts = [a4, b4, a1, a3, b1, b3]

    st0, cnorm, *w0, top0 = local_weights(pos, centroids, pts[:2])
    st1, *w1, top1 = local_weights(pos, centroids, pts[2:6], cnorm)
    a2, b2, stats, *w2, top2 = local_weights(pos, centroids, last, cnorm, (st0, st1))
    pts += [a2, b2]

    every = lax.all_to_all(stats, "cent", 0, 0)

    weights = list(zip(w0, w1, w2))
    *sums0, partition, rows = chunk_sums(pos, 0, weights[0], pts, (every, top0, top1, top2))
    sums1 = chunk_sums(pos, 1, weights[1], pts, (rows,))
    got0 = lax.ppermute(sums0[0], "dp", TO_CORE)
    got1 = lax.ppermute(sums1[0], "dp", TO_CORE)
    packed0, counts0 = pack(pos, sums0[0], sums0[1], got0, (sums1[0],))
    packed1, counts1, row = pack(pos, sums1[0], sums1[1], got1, (), (counts0,))
    far = [lax.ppermute(p.astype(jnp.float16), "dp", TO_Y) for p in (packed0, packed1)]
    far_row = lax.ppermute(row, "dp", TO_Y)

    near_got = [lax.ppermute(s[2], "dp", TO_CORE) for s in (sums0, sums1)]
    (near,) = call(
        near_body,
        "near",
        pos,
        (sums0[3], sums1[3], *near_got, centroids),
        (f32(K_DEV, WIDTH),),
        after=(packed1,),
    )
    far = [f.astype(jnp.float32) for f in far]
    args = (near, counts0, counts1, far_row, *far)
    scratch = [pltpu.VMEM((K_DEV, WIDTH), jnp.bfloat16), pltpu.SemaphoreType.DMA((2,))]
    out = (bf16(K_DEV, WIDTH),)
    (fresh,) = call(fresh_body, "fresh", pos, args, out, scratch, far_outs=1)

    mine = 4 * z + x
    own_rows = jnp.concatenate(
        [
            lax.dynamic_slice(partition, (mine, y_lo * half + UNIT * i), (1, half))[0]
            for i in range(2)
        ]
    )
    return fresh, own_rows


def solution(mesh):
    placed = (P(("dp", "cent"), None), P("cent", None))
    return jax.shard_map(
        on_device,
        mesh=mesh,
        in_specs=placed,
        out_specs=(P("cent", "dp"), P(("dp", "cent"))),
        check_vma=False,
    )
```

```python
import functools

import jax
import jax.numpy as jnp
from jax import lax
from jax.experimental import pallas as pl
from jax.experimental.pallas import tpu as pltpu
from jax.sharding import PartitionSpec as P

D = 1024
PTS_DEV = 64
N_CENT = 32
K_DEV = 1568
ROWS = PTS_DEV * N_CENT
WIDTH = D // 4
HALF = K_DEV // 2
SCALE = 1.0 / D**0.5
VMEM = 8 * 1024 * 1024
SPAN = 256.0

STEPS = (0, 1, 3, 2)
PIECES = tuple(
    tuple(("a", d, s) if part == "a" else ("b", s, d) for s in STEPS)
    for part, d in (
        ("a", 0), ("b", 0),
        ("a", 1), ("a", 3), ("b", 1), ("b", 3),
        ("a", 2), ("b", 2),
    )
)
UNIT = PTS_DEV
PIECE = 4 * UNIT
BLOCKS = 16


def block_of(unit, z, x):
    _, dz, dx = unit
    return (z ^ dz) * 4 + (x ^ dx)


def low_lanes():
    return lax.broadcasted_iota(jnp.int32, (8, 128), 1) < UNIT


IN_VMEM = pl.BlockSpec(memory_space=pltpu.VMEM)
IN_SMEM = pl.BlockSpec(memory_space=pltpu.SMEM)
IN_HBM = pl.BlockSpec(memory_space=pltpu.HBM)
ANYWHERE = pl.BlockSpec(memory_space=pl.ANY)


def call(body, name, pos, args, outs, scratch=(), flops=0, exps=0, far_args=(), after=(), far_outs=0):
    moved = sum(a.size * a.dtype.itemsize for a in (*args, *far_args, *outs))
    near = len(outs) - far_outs
    n = len(after)
    return pl.pallas_call(
        lambda p, *refs: body(p, *refs[n:]),
        in_specs=[IN_SMEM]
        + [ANYWHERE] * n
        + [IN_VMEM] * len(args)
        + [IN_HBM] * len(far_args),
        out_specs=[IN_VMEM] * near + [IN_HBM] * far_outs,
        out_shape=list(outs),
        scratch_shapes=list(scratch),
        compiler_params=pltpu.CompilerParams(vmem_limit_bytes=VMEM),
        cost_estimate=pl.CostEstimate(flops=flops, bytes_accessed=moved, transcendentals=exps),
        name=name,
    )(pos, *after, *args, *far_args)


def f32(*shape):
    return jax.ShapeDtypeStruct(shape, jnp.float32)


def bf16(*shape):
    return jax.ShapeDtypeStruct(shape, jnp.bfloat16)


def join_body(pos, *refs):
    ins, outs = refs[:-2], refs[-2:]
    n = len(ins) // 2
    for k, out in enumerate(outs):
        at = 0
        for ref in ins[k * n : (k + 1) * n]:
            out[at : at + ref.shape[0], :] = ref[...]
            at += ref.shape[0]


def join(pos, a, b):
    return call(join_body, "join", pos, (*a, *b), (bf16(PIECE, D), bf16(PIECE, D)))


def logits_body(n, units, prior, pos, *refs):
    cent, pts, before, refs = refs[0], refs[1 : 1 + n], refs[1 + n : 1 + n + prior], refs[1 + n + prior :]
    if prior:
        cnorm, *joined, out, weights0, weights1, tops, place = refs
        weights = (weights0, weights1)
        mid = PIECE // 2
        for i, ref in enumerate(pts):
            joined[i // 2][i % 2 * mid : (i % 2 + 1) * mid, :] = ref[...]
        n, pts = n // 2, joined
    elif units:
        cnorm, out, *weights, tops = refs
    else:
        out, cnorm, *weights, tops = refs
        for j in range(2):
            here = slice(j * HALF, (j + 1) * HALF)
            wide = cent[here, :].astype(jnp.float32)
            cnorm[here, :] = jnp.sum(wide * wide, axis=1, keepdims=True)
    low = low_lanes()
    rows = []
    for i in range(n):
        cols = slice(i * PIECE, (i + 1) * PIECE)
        top, total = [], []
        for j in range(2):
            here = slice(j * HALF, (j + 1) * HALF)
            cross = lax.dot_general(
                cent[here, :],
                pts[i][...],
                (((1,), (1,)), ((), ())),
                preferred_element_type=jnp.float32,
            )
            part = (2.0 * cross - cnorm[here, :]) * SCALE
            top.append(jnp.max(part, axis=0, keepdims=True))
            part = jnp.exp(part - top[j])
            weights[j][:, cols] = part
            tops[j : j + 1, cols] = top[j]
            total.append(jnp.sum(part, axis=0, keepdims=True))
        peak = jnp.maximum(top[0], top[1])
        whole = total[0] * jnp.exp(top[0] - peak) + total[1] * jnp.exp(top[1] - peak)
        logs = peak + jnp.log(whole)
        for h in range(2):
            rows.append(logs[:, h * 128 : (h + 1) * 128])
    if not prior:
        for i, row in enumerate(rows):
            out[i : i + 1, :] = row
    else:
        all_rows = [b[i : i + 1, :] for b in before for i in range(b.shape[0])] + rows
        for i, row in enumerate(all_rows):
            straight = jnp.broadcast_to(row, (8, 128))
            turned = pltpu.roll(straight, UNIT, 1)
            for h in range(2):
                unit = units[2 * i + h]
                a = unit[0] == "a"
                value = straight if (h == 0) == a else turned
                lanes = slice(0, UNIT) if a else slice(UNIT, 128)
                place[pl.ds(block_of(unit, pos[0], pos[1]), 1), lanes] = value[0:1, lanes]
        whole = place[...]
        for j in range(N_CENT):
            out[j] = whole


def local_weights(pos, centroids, pts, cnorm=None, before=()):
    m = len(pts)
    n = m // 2 if before else m
    units = sum(PIECES, ()) if cnorm is not None else ()
    stats = f32(N_CENT, BLOCKS, 128) if before else f32(2 * n, 128)
    args = (centroids, *pts, *before) + (() if cnorm is None else (cnorm,))
    outs = (stats,) + ((f32(K_DEV, 1),) if cnorm is None else ())
    if before:
        outs = (bf16(PIECE, D), bf16(PIECE, D), stats)
    outs += (f32(HALF, n * PIECE), f32(HALF, n * PIECE), f32(2, n * PIECE))
    return call(
        functools.partial(logits_body, m, units, len(before)),
        "weights",
        pos,
        args,
        outs,
        [pltpu.VMEM((BLOCKS, 128), jnp.float32)] if before else [],
        flops=2 * K_DEV * n * PIECE * D,
        exps=K_DEV * n * PIECE,
    )


def merge_stats(pos, every, tops, place, turned, rows):
    low = low_lanes()[0:1]
    peak = every[0]
    for j in range(1, N_CENT):
        peak = jnp.maximum(peak, every[j])
    total = jnp.zeros_like(peak)
    for j in range(N_CENT):
        total = total + jnp.exp(every[j] - peak)
    both = []
    for value in (peak, 1.0 / total):
        place[...] = value
        turned[...] = pltpu.roll(value, UNIT, 1)
        parts = []
        for units in PIECES:
            for h in range(2):
                pair = units[2 * h : 2 * h + 2]
                refs = (place, turned) if pair[0][0] == "a" else (turned, place)
                first, second = (
                    ref[pl.ds(block_of(unit, pos[0], pos[1]), 1), :]
                    for ref, unit in zip(refs, pair)
                )
                parts.append(jnp.where(low, first, second))
        both.append(parts)
    at = 0
    for ref in tops:
        for h in range(ref.shape[1] // 128):
            lanes = slice(h * 128, (h + 1) * 128)
            rows[0:2, at * 128 : (at + 1) * 128] = jnp.exp(ref[:, lanes] - both[0][at]) * both[1][at]
            at += 1
    return peak + jnp.log(total)


def columns(pos, which):
    return pl.ds(pl.multiple_of(pos[which] * WIDTH, WIDTH), WIDTH)


def sums_body(chunk, pos, *refs):
    weights, pts, refs = refs[:3], refs[3:11], refs[11:]
    if chunk == 0:
        every, tops, sums = refs[0], refs[1:4], refs[4:8]
        partition, rows, resp, place, turned = refs[8:]
        partition[...] = merge_stats(pos, every, tops, place, turned, rows)
    else:
        rows, sums, resp = refs[0], refs[1:5], refs[5]
    cnt, p = None, 0
    for ref in weights:
        for j in range(ref.shape[1] // PIECE):
            here = slice(p * PIECE, (p + 1) * PIECE)
            part = ref[:, j * PIECE : (j + 1) * PIECE]
            r = (part * rows[chunk : chunk + 1, here]).astype(jnp.bfloat16)
            resp[:, here] = r
            wide = r.astype(jnp.float32)
            two = wide[:, :128] + wide[:, 128:]
            cnt = cnt + two if p else two
            p += 1
    for k in range(4):
        acc = None
        for p in range(8):
            d = jnp.dot(
                resp[:, p * PIECE : (p + 1) * PIECE],
                pts[p][:, columns(pos, 2 + k)],
                preferred_element_type=jnp.float32,
            )
            acc = acc + d if p else d
        sums[k][:, :WIDTH] = acc
    sums[0][:, WIDTH:] = jnp.broadcast_to(jnp.sum(cnt, axis=1, keepdims=True), (HALF, 128))


def chunk_sums(pos, chunk, weights, pts, stats):
    outs = [f32(HALF, WIDTH + 128)] + [f32(HALF, WIDTH)] * 3
    scratch = [pltpu.VMEM((HALF, ROWS), jnp.bfloat16)]
    if chunk == 0:
        outs += [f32(BLOCKS, 128), f32(8, ROWS)]
        scratch += [pltpu.VMEM((BLOCKS, 128), jnp.float32)] * 2
    return call(
        functools.partial(sums_body, chunk),
        "sums",
        pos,
        (*weights, *pts, *stats),
        outs,
        scratch,
        flops=2 * HALF * ROWS * D,
    )


def one_hot(shape):
    return (lax.broadcasted_iota(jnp.int32, shape, 0) == 0).astype(jnp.float32)


def pack_body(pos, first, second, got, *refs):
    cnt = first[:, WIDTH:] + got[:, WIDTH:]
    packed, counts = refs[1:3] if len(refs) > 2 else refs
    counts[...] = cnt
    factor = SPAN / (cnt + 0.25)
    for k in range(2):
        lanes = slice(k * 128, (k + 1) * 128)
        packed[:, lanes] = (second[:, lanes] + got[:, lanes]) * factor
    if len(refs) > 2:
        for c, here in enumerate((refs[0][...], cnt)):
            refs[3][8 * c : 8 * (c + 1), :] = lax.dot_general(
                one_hot((128, 8)),
                here,
                (((0,), (1,)), ((), ())),
                precision=lax.Precision.HIGHEST,
                preferred_element_type=jnp.float32,
            )


def pack(pos, first, second, got, after, before=()):
    outs = (f32(HALF, WIDTH), f32(HALF, 128)) + ((f32(16, HALF),) if before else ())
    return call(pack_body, "pack", pos, (first, second, got, *before), outs, after=after)


def near_body(pos, *refs):
    cent, near = refs[4:]
    for c in range(2):
        here = slice(c * HALF, (c + 1) * HALF)
        for k in range(2):
            lanes = slice(k * 128, (k + 1) * 128)
            own = cent[here, pl.ds(pl.multiple_of(pos[6] * WIDTH + k * 128, 128), 128)]
            total = refs[c][:, lanes] + refs[2 + c][:, lanes]
            near[here, lanes] = total + 0.25 * own.astype(jnp.float32)


def fresh_body(pos, near, counts0, counts1, far_row, far0, far1, fresh, out, sem):
    copies = []
    for c, (counts, far) in enumerate(((counts0, far0), (counts1, far1))):
        here = slice(c * HALF, (c + 1) * HALF)
        far_counts = lax.dot_general(
            far_row[8 * c : 8 * (c + 1), :],
            one_hot((8, 128)),
            (((0,), (0,)), ((), ())),
            precision=lax.Precision.HIGHEST,
            preferred_element_type=jnp.float32,
        )
        weight = 1.0 / (counts[...] + far_counts + 0.25)
        factor = (far_counts + 0.25) * (1.0 / SPAN)
        for k in range(2):
            lanes = slice(k * 128, (k + 1) * 128)
            total = near[here, lanes] + far[:, lanes] * factor
            out[here, lanes] = (total * weight).astype(out.dtype)
        copies.append(pltpu.make_async_copy(out.at[here], fresh.at[here], sem.at[c]))
        copies[c].start()
    for c in copies:
        c.wait()


FROM_PAIR = [(i, i ^ 1) for i in range(N_CENT)]


def from_x(d):
    return [(i, i ^ 2 * d) for i in range(N_CENT)]


def from_z(d):
    return [(i, i ^ 8 * d) for i in range(N_CENT)]


TO_CORE = [(i, i ^ 1) for i in range(4)]
TO_Y = [(i, i ^ 2) for i in range(4)]


def on_device(points, centroids):
    dp, cent = lax.axis_index("dp"), lax.axis_index("cent")
    core, y_hi = dp % 2, dp // 2
    z, x, y_lo = cent // 8, cent // 2 % 4, cent % 2
    far, near = 2 * (1 - y_hi), 2 * y_hi
    pos = jnp.stack([z, x, far + 1 - core, far + core, near + 1 - core, near + core, dp])

    other = lax.ppermute(points, "cent", FROM_PAIR)
    half = PTS_DEV // 2
    first = jnp.where(y_lo == 0, points, other)
    second = jnp.where(y_lo == 0, other, points)
    a = jnp.concatenate([first[:half], second[:half]])
    b = jnp.concatenate([first[half:], second[half:]])
    a4, b4 = join(
        pos,
        [a] + [lax.ppermute(a, "cent", from_x(d)) for d in STEPS[1:]],
        [b] + [lax.ppermute(b, "cent", from_z(d)) for d in STEPS[1:]],
    )
    a1, b1 = lax.ppermute(a4, "cent", from_z(1)), lax.ppermute(b4, "cent", from_x(1))
    a3, b3 = lax.ppermute(a4, "cent", from_z(3)), lax.ppermute(b4, "cent", from_x(3))
    mid = PIECE // 2
    last = [
        lax.ppermute(a3[:mid], "cent", from_z(1)),
        lax.ppermute(a1[mid:], "cent", from_z(3)),
        lax.ppermute(b3[:mid], "cent", from_x(1)),
        lax.ppermute(b1[mid:], "cent", from_x(3)),
    ]
    pts = [a4, b4, a1, a3, b1, b3]

    st0, cnorm, *w0, top0 = local_weights(pos, centroids, pts[:2])
    st1, *w1, top1 = local_weights(pos, centroids, pts[2:6], cnorm)
    a2, b2, stats, *w2, top2 = local_weights(pos, centroids, last, cnorm, (st0, st1))
    pts += [a2, b2]

    every = lax.all_to_all(stats, "cent", 0, 0)

    weights = list(zip(w0, w1, w2))
    *sums0, partition, rows = chunk_sums(pos, 0, weights[0], pts, (every, top0, top1, top2))
    sums1 = chunk_sums(pos, 1, weights[1], pts, (rows,))
    got0 = lax.ppermute(sums0[0], "dp", TO_CORE)
    got1 = lax.ppermute(sums1[0], "dp", TO_CORE)
    packed0, counts0 = pack(pos, sums0[0], sums0[1], got0, (sums1[0],))
    moved0 = lax.optimization_barrier(packed0.astype(jnp.float16))
    after = (moved0[:8, :128].astype(jnp.float32),)
    packed1, counts1, row = pack(pos, sums1[0], sums1[1], got1, after, (counts0,))
    far = [lax.ppermute(m, "dp", TO_Y) for m in (moved0, packed1.astype(jnp.float16))]
    far_row = lax.ppermute(row, "dp", TO_Y)

    near_got = [lax.ppermute(s[2], "dp", TO_CORE) for s in (sums0, sums1)]
    (near,) = call(
        near_body,
        "near",
        pos,
        (sums0[3], sums1[3], *near_got, centroids),
        (f32(K_DEV, WIDTH),),
        after=(packed1,),
    )
    far = [f.astype(jnp.float32) for f in far]
    args = (near, counts0, counts1, far_row, *far)
    scratch = [pltpu.VMEM((K_DEV, WIDTH), jnp.bfloat16), pltpu.SemaphoreType.DMA((2,))]
    out = (bf16(K_DEV, WIDTH),)
    (fresh,) = call(fresh_body, "fresh", pos, args, out, scratch, far_outs=1)

    mine = 4 * z + x
    own_rows = jnp.concatenate(
        [
            lax.dynamic_slice(partition, (mine, y_lo * half + UNIT * i), (1, half))[0]
            for i in range(2)
        ]
    )
    return fresh, own_rows


def solution(mesh):
    placed = (P(("dp", "cent"), None), P("cent", None))
    return jax.shard_map(
        on_device,
        mesh=mesh,
        in_specs=placed,
        out_specs=(P("cent", "dp"), P(("dp", "cent"))),
        check_vma=False,
    )
```

```python
import functools

import jax
import jax.numpy as jnp
from jax import lax
from jax.experimental import pallas as pl
from jax.experimental.pallas import tpu as pltpu
from jax.sharding import PartitionSpec as P

D = 1024
PTS_DEV = 64
N_CENT = 32
K_DEV = 1568
ROWS = PTS_DEV * N_CENT
WIDTH = D // 4
HALF = K_DEV // 2
SCALE = 1.0 / D**0.5
VMEM = 8 * 1024 * 1024
SPAN = 256.0

STEPS = (0, 1, 3, 2)
PIECES = tuple(
    tuple(("a", d, s) if part == "a" else ("b", s, d) for s in STEPS)
    for part, d in (
        ("a", 0), ("b", 0),
        ("a", 1), ("a", 3), ("b", 1), ("b", 3),
        ("a", 2), ("b", 2),
    )
)
UNIT = PTS_DEV
PIECE = 4 * UNIT
BLOCKS = 16


def block_of(unit, z, x):
    _, dz, dx = unit
    return (z ^ dz) * 4 + (x ^ dx)


def low_lanes():
    return lax.broadcasted_iota(jnp.int32, (8, 128), 1) < UNIT


IN_VMEM = pl.BlockSpec(memory_space=pltpu.VMEM)
IN_SMEM = pl.BlockSpec(memory_space=pltpu.SMEM)
IN_HBM = pl.BlockSpec(memory_space=pltpu.HBM)
ANYWHERE = pl.BlockSpec(memory_space=pl.ANY)


def call(body, name, pos, args, outs, scratch=(), flops=0, exps=0, far_args=(), after=(), far_outs=0):
    moved = sum(a.size * a.dtype.itemsize for a in (*args, *far_args, *outs))
    near = len(outs) - far_outs
    n = len(after)
    return pl.pallas_call(
        lambda p, *refs: body(p, *refs[n:]),
        in_specs=[IN_SMEM]
        + [ANYWHERE] * n
        + [IN_VMEM] * len(args)
        + [IN_HBM] * len(far_args),
        out_specs=[IN_VMEM] * near + [IN_HBM] * far_outs,
        out_shape=list(outs),
        scratch_shapes=list(scratch),
        compiler_params=pltpu.CompilerParams(vmem_limit_bytes=VMEM),
        cost_estimate=pl.CostEstimate(flops=flops, bytes_accessed=moved, transcendentals=exps),
        name=name,
    )(pos, *after, *args, *far_args)


def f32(*shape):
    return jax.ShapeDtypeStruct(shape, jnp.float32)


def bf16(*shape):
    return jax.ShapeDtypeStruct(shape, jnp.bfloat16)


def join_body(pos, *refs):
    ins, outs = refs[:-2], refs[-2:]
    n = len(ins) // 2
    for k, out in enumerate(outs):
        at = 0
        for ref in ins[k * n : (k + 1) * n]:
            out[at : at + ref.shape[0], :] = ref[...]
            at += ref.shape[0]


def join(pos, a, b):
    return call(join_body, "join", pos, (*a, *b), (bf16(PIECE, D), bf16(PIECE, D)))


def logits_body(n, units, prior, pos, *refs):
    cent, pts, before, refs = refs[0], refs[1 : 1 + n], refs[1 + n : 1 + n + prior], refs[1 + n + prior :]
    if prior:
        cnorm, *joined, out, weights0, weights1, tops, place = refs
        weights = (weights0, weights1)
        mid = PIECE // 2
        for i, ref in enumerate(pts):
            joined[i // 2][i % 2 * mid : (i % 2 + 1) * mid, :] = ref[...]
        n, pts = n // 2, joined
    elif units:
        cnorm, out, *weights, tops = refs
    else:
        out, cnorm, *weights, tops = refs
        for j in range(2):
            here = slice(j * HALF, (j + 1) * HALF)
            wide = cent[here, :].astype(jnp.float32)
            cnorm[here, :] = jnp.sum(wide * wide, axis=1, keepdims=True)
    low = low_lanes()
    rows = []
    for i in range(n):
        cols = slice(i * PIECE, (i + 1) * PIECE)
        top, total = [], []
        for j in range(2):
            here = slice(j * HALF, (j + 1) * HALF)
            cross = lax.dot_general(
                cent[here, :],
                pts[i][...],
                (((1,), (1,)), ((), ())),
                preferred_element_type=jnp.float32,
            )
            part = (2.0 * cross - cnorm[here, :]) * SCALE
            top.append(jnp.max(part, axis=0, keepdims=True))
            part = jnp.exp(part - top[j])
            weights[j][:, cols] = part
            tops[j : j + 1, cols] = top[j]
            total.append(jnp.sum(part, axis=0, keepdims=True))
        peak = jnp.maximum(top[0], top[1])
        whole = total[0] * jnp.exp(top[0] - peak) + total[1] * jnp.exp(top[1] - peak)
        logs = peak + jnp.log(whole)
        for h in range(2):
            rows.append(logs[:, h * 128 : (h + 1) * 128])
    if not prior:
        for i, row in enumerate(rows):
            out[i : i + 1, :] = row
    else:
        all_rows = [b[i : i + 1, :] for b in before for i in range(b.shape[0])] + rows
        for i, row in enumerate(all_rows):
            straight = jnp.broadcast_to(row, (8, 128))
            turned = pltpu.roll(straight, UNIT, 1)
            for h in range(2):
                unit = units[2 * i + h]
                a = unit[0] == "a"
                value = straight if (h == 0) == a else turned
                lanes = slice(0, UNIT) if a else slice(UNIT, 128)
                place[pl.ds(block_of(unit, pos[0], pos[1]), 1), lanes] = value[0:1, lanes]
        whole = place[...]
        for j in range(N_CENT):
            out[j] = whole


def local_weights(pos, centroids, pts, cnorm=None, before=()):
    m = len(pts)
    n = m // 2 if before else m
    units = sum(PIECES, ()) if cnorm is not None else ()
    stats = f32(N_CENT, BLOCKS, 128) if before else f32(2 * n, 128)
    args = (centroids, *pts, *before) + (() if cnorm is None else (cnorm,))
    outs = (stats,) + ((f32(K_DEV, 1),) if cnorm is None else ())
    if before:
        outs = (bf16(PIECE, D), bf16(PIECE, D), stats)
    outs += (f32(HALF, n * PIECE), f32(HALF, n * PIECE), f32(2, n * PIECE))
    return call(
        functools.partial(logits_body, m, units, len(before)),
        "weights",
        pos,
        args,
        outs,
        [pltpu.VMEM((BLOCKS, 128), jnp.float32)] if before else [],
        flops=2 * K_DEV * n * PIECE * D,
        exps=K_DEV * n * PIECE,
    )


def merge_stats(pos, every, tops, place, turned, rows):
    low = low_lanes()[0:1]
    peak = every[0]
    for j in range(1, N_CENT):
        peak = jnp.maximum(peak, every[j])
    total = jnp.zeros_like(peak)
    for j in range(N_CENT):
        total = total + jnp.exp(every[j] - peak)
    both = []
    for value in (peak, 1.0 / total):
        place[...] = value
        turned[...] = pltpu.roll(value, UNIT, 1)
        parts = []
        for units in PIECES:
            for h in range(2):
                pair = units[2 * h : 2 * h + 2]
                refs = (place, turned) if pair[0][0] == "a" else (turned, place)
                first, second = (
                    ref[pl.ds(block_of(unit, pos[0], pos[1]), 1), :]
                    for ref, unit in zip(refs, pair)
                )
                parts.append(jnp.where(low, first, second))
        both.append(parts)
    at = 0
    for ref in tops:
        for h in range(ref.shape[1] // 128):
            lanes = slice(h * 128, (h + 1) * 128)
            rows[0:2, at * 128 : (at + 1) * 128] = jnp.exp(ref[:, lanes] - both[0][at]) * both[1][at]
            at += 1
    return peak + jnp.log(total)


def columns(pos, which):
    return pl.ds(pl.multiple_of(pos[which] * WIDTH, WIDTH), WIDTH)


def sums_body(chunk, pos, *refs):
    weights, pts, refs = refs[:3], refs[3:11], refs[11:]
    if chunk == 0:
        every, tops, sums = refs[0], refs[1:4], refs[4:8]
        partition, rows, resp, place, turned = refs[8:]
        partition[...] = merge_stats(pos, every, tops, place, turned, rows)
    else:
        rows, sums, resp = refs[0], refs[1:5], refs[5]
    cnt, p = None, 0
    for ref in weights:
        for j in range(ref.shape[1] // PIECE):
            here = slice(p * PIECE, (p + 1) * PIECE)
            part = ref[:, j * PIECE : (j + 1) * PIECE]
            r = (part * rows[chunk : chunk + 1, here]).astype(jnp.bfloat16)
            resp[:, here] = r
            wide = r.astype(jnp.float32)
            two = wide[:, :128] + wide[:, 128:]
            cnt = cnt + two if p else two
            p += 1
    for k in range(4):
        acc = None
        for p in range(8):
            d = jnp.dot(
                resp[:, p * PIECE : (p + 1) * PIECE],
                pts[p][:, columns(pos, 2 + k)],
                preferred_element_type=jnp.float32,
            )
            acc = acc + d if p else d
        sums[k][:, :WIDTH] = acc
    sums[0][:, WIDTH:] = jnp.broadcast_to(jnp.sum(cnt, axis=1, keepdims=True), (HALF, 128))


def chunk_sums(pos, chunk, weights, pts, stats):
    outs = [f32(HALF, WIDTH + 128)] + [f32(HALF, WIDTH)] * 3
    scratch = [pltpu.VMEM((HALF, ROWS), jnp.bfloat16)]
    if chunk == 0:
        outs += [f32(BLOCKS, 128), f32(8, ROWS)]
        scratch += [pltpu.VMEM((BLOCKS, 128), jnp.float32)] * 2
    return call(
        functools.partial(sums_body, chunk),
        "sums",
        pos,
        (*weights, *pts, *stats),
        outs,
        scratch,
        flops=2 * HALF * ROWS * D,
    )


def one_hot(shape):
    return (lax.broadcasted_iota(jnp.int32, shape, 0) == 0).astype(jnp.float32)


def pack_body(pos, first, second, got, *refs):
    packed, counts, row = refs[-3:]
    cnt = first[:, WIDTH:] + got[:, WIDTH:]
    counts[...] = cnt
    here = lax.dot_general(
        one_hot((128, 8)),
        cnt,
        (((0,), (1,)), ((), ())),
        precision=lax.Precision.HIGHEST,
        preferred_element_type=jnp.float32,
    )
    if len(refs) > 3:
        row[:8, :] = refs[0][...]
        row[8:, :] = here
    else:
        row[...] = here
    factor = SPAN / (cnt + 0.25)
    for k in range(2):
        lanes = slice(k * 128, (k + 1) * 128)
        packed[:, lanes] = (second[:, lanes] + got[:, lanes]) * factor


def pack(pos, first, second, got, after, before=()):
    outs = (f32(HALF, WIDTH), f32(HALF, 128), f32(16 if before else 8, HALF))
    return call(pack_body, "pack", pos, (first, second, got, *before), outs, after=after)


def near_body(pos, *refs):
    cent, near = refs[4:]
    for c in range(2):
        here = slice(c * HALF, (c + 1) * HALF)
        for k in range(2):
            lanes = slice(k * 128, (k + 1) * 128)
            own = cent[here, pl.ds(pl.multiple_of(pos[6] * WIDTH + k * 128, 128), 128)]
            total = refs[c][:, lanes] + refs[2 + c][:, lanes]
            near[here, lanes] = total + 0.25 * own.astype(jnp.float32)


def fresh_body(pos, near, counts0, counts1, far_row, far0, far1, out):
    for c, (counts, far) in enumerate(((counts0, far0), (counts1, far1))):
        here = slice(c * HALF, (c + 1) * HALF)
        far_counts = lax.dot_general(
            far_row[8 * c : 8 * (c + 1), :],
            one_hot((8, 128)),
            (((0,), (0,)), ((), ())),
            precision=lax.Precision.HIGHEST,
            preferred_element_type=jnp.float32,
        )
        weight = 1.0 / (counts[...] + far_counts + 0.25)
        factor = (far_counts + 0.25) * (1.0 / SPAN)
        for k in range(2):
            lanes = slice(k * 128, (k + 1) * 128)
            total = near[here, lanes] + far[:, lanes] * factor
            out[here, lanes] = (total * weight).astype(out.dtype)


FROM_PAIR = [(i, i ^ 1) for i in range(N_CENT)]


def from_x(d):
    return [(i, i ^ 2 * d) for i in range(N_CENT)]


def from_z(d):
    return [(i, i ^ 8 * d) for i in range(N_CENT)]


TO_CORE = [(i, i ^ 1) for i in range(4)]
TO_Y = [(i, i ^ 2) for i in range(4)]


def on_device(points, centroids):
    dp, cent = lax.axis_index("dp"), lax.axis_index("cent")
    core, y_hi = dp % 2, dp // 2
    z, x, y_lo = cent // 8, cent // 2 % 4, cent % 2
    far, near = 2 * (1 - y_hi), 2 * y_hi
    pos = jnp.stack([z, x, far + 1 - core, far + core, near + 1 - core, near + core, dp])

    other = lax.ppermute(points, "cent", FROM_PAIR)
    half = PTS_DEV // 2
    first = jnp.where(y_lo == 0, points, other)
    second = jnp.where(y_lo == 0, other, points)
    a = jnp.concatenate([first[:half], second[:half]])
    b = jnp.concatenate([first[half:], second[half:]])
    a4, b4 = join(
        pos,
        [a] + [lax.ppermute(a, "cent", from_x(d)) for d in STEPS[1:]],
        [b] + [lax.ppermute(b, "cent", from_z(d)) for d in STEPS[1:]],
    )
    a1, b1 = lax.ppermute(a4, "cent", from_z(1)), lax.ppermute(b4, "cent", from_x(1))
    a3, b3 = lax.ppermute(a4, "cent", from_z(3)), lax.ppermute(b4, "cent", from_x(3))
    mid = PIECE // 2
    last = [
        lax.ppermute(a3[:mid], "cent", from_z(1)),
        lax.ppermute(a1[mid:], "cent", from_z(3)),
        lax.ppermute(b3[:mid], "cent", from_x(1)),
        lax.ppermute(b1[mid:], "cent", from_x(3)),
    ]
    pts = [a4, b4, a1, a3, b1, b3]

    st0, cnorm, *w0, top0 = local_weights(pos, centroids, pts[:2])
    st1, *w1, top1 = local_weights(pos, centroids, pts[2:6], cnorm)
    a2, b2, stats, *w2, top2 = local_weights(pos, centroids, last, cnorm, (st0, st1))
    pts += [a2, b2]

    every = lax.all_to_all(stats, "cent", 0, 0)

    weights = list(zip(w0, w1, w2))
    *sums0, partition, rows = chunk_sums(pos, 0, weights[0], pts, (every, top0, top1, top2))
    sums1 = chunk_sums(pos, 1, weights[1], pts, (rows,))
    got0 = lax.ppermute(sums0[0], "dp", TO_CORE)
    got1 = lax.ppermute(sums1[0], "dp", TO_CORE)
    packed0, counts0, row = pack(pos, sums0[0], sums0[1], got0, (sums1[0],))
    packed1, counts1, row = pack(pos, sums1[0], sums1[1], got1, (), (row,))
    far = [lax.ppermute(p.astype(jnp.float16), "dp", TO_Y) for p in (packed0, packed1)]
    far_row = lax.ppermute(row, "dp", TO_Y)

    near_got = [lax.ppermute(s[2], "dp", TO_CORE) for s in (sums0, sums1)]
    (near,) = call(
        near_body,
        "near",
        pos,
        (sums0[3], sums1[3], *near_got, centroids),
        (f32(K_DEV, WIDTH),),
        after=(packed1,),
    )
    far = [f.astype(jnp.float32) for f in far]
    args = (near, counts0, counts1, far_row, *far)
    (fresh,) = call(fresh_body, "fresh", pos, args, (bf16(K_DEV, WIDTH),))

    mine = 4 * z + x
    own_rows = jnp.concatenate(
        [
            lax.dynamic_slice(partition, (mine, y_lo * half + UNIT * i), (1, half))[0]
            for i in range(2)
        ]
    )
    return fresh, own_rows


def solution(mesh):
    placed = (P(("dp", "cent"), None), P("cent", None))
    return jax.shard_map(
        on_device,
        mesh=mesh,
        in_specs=placed,
        out_specs=(P("cent", "dp"), P(("dp", "cent"))),
        check_vma=False,
    )
```

```python
import functools

import jax
import jax.numpy as jnp
from jax import lax
from jax.experimental import pallas as pl
from jax.experimental.pallas import tpu as pltpu
from jax.sharding import PartitionSpec as P

D = 1024
PTS_DEV = 64
N_CENT = 32
K_DEV = 1568
ROWS = PTS_DEV * N_CENT
WIDTH = D // 4
HALF = K_DEV // 2
SCALE = 1.0 / D**0.5
VMEM = 8 * 1024 * 1024
SPAN = 256.0

STEPS = (0, 1, 3, 2)
PIECES = tuple(
    tuple(("a", d, s) if part == "a" else ("b", s, d) for s in STEPS)
    for part, d in (
        ("a", 0), ("b", 0),
        ("a", 1), ("a", 3), ("b", 1), ("b", 3),
        ("a", 2), ("b", 2),
    )
)
UNIT = PTS_DEV
PIECE = 4 * UNIT
BLOCKS = 16


def block_of(unit, z, x):
    _, dz, dx = unit
    return (z ^ dz) * 4 + (x ^ dx)


def low_lanes():
    return lax.broadcasted_iota(jnp.int32, (8, 128), 1) < UNIT


IN_VMEM = pl.BlockSpec(memory_space=pltpu.VMEM)
IN_SMEM = pl.BlockSpec(memory_space=pltpu.SMEM)
IN_HBM = pl.BlockSpec(memory_space=pltpu.HBM)
ANYWHERE = pl.BlockSpec(memory_space=pl.ANY)


def call(body, name, pos, args, outs, scratch=(), flops=0, exps=0, far_args=(), after=(), far_outs=0):
    moved = sum(a.size * a.dtype.itemsize for a in (*args, *far_args, *outs))
    near = len(outs) - far_outs
    n = len(after)
    return pl.pallas_call(
        lambda p, *refs: body(p, *refs[n:]),
        in_specs=[IN_SMEM]
        + [ANYWHERE] * n
        + [IN_VMEM] * len(args)
        + [IN_HBM] * len(far_args),
        out_specs=[IN_VMEM] * near + [IN_HBM] * far_outs,
        out_shape=list(outs),
        scratch_shapes=list(scratch),
        compiler_params=pltpu.CompilerParams(vmem_limit_bytes=VMEM),
        cost_estimate=pl.CostEstimate(flops=flops, bytes_accessed=moved, transcendentals=exps),
        name=name,
    )(pos, *after, *args, *far_args)


def f32(*shape):
    return jax.ShapeDtypeStruct(shape, jnp.float32)


def bf16(*shape):
    return jax.ShapeDtypeStruct(shape, jnp.bfloat16)


def join_body(pos, *refs):
    ins, outs = refs[:-2], refs[-2:]
    n = len(ins) // 2
    for k, out in enumerate(outs):
        at = 0
        for ref in ins[k * n : (k + 1) * n]:
            out[at : at + ref.shape[0], :] = ref[...]
            at += ref.shape[0]


def join(pos, a, b):
    return call(join_body, "join", pos, (*a, *b), (bf16(PIECE, D), bf16(PIECE, D)))


def logits_body(n, units, prior, pos, *refs):
    cent, pts, before, refs = refs[0], refs[1 : 1 + n], refs[1 + n : 1 + n + prior], refs[1 + n + prior :]
    if prior:
        cnorm, *joined, out, weights0, weights1, tops, place = refs
        weights = (weights0, weights1)
        mid = PIECE // 2
        for i, ref in enumerate(pts):
            joined[i // 2][i % 2 * mid : (i % 2 + 1) * mid, :] = ref[...]
        n, pts = n // 2, joined
    elif units:
        cnorm, out, *weights, tops = refs
    else:
        out, cnorm, *weights, tops = refs
        for j in range(2):
            here = slice(j * HALF, (j + 1) * HALF)
            wide = cent[here, :].astype(jnp.float32)
            cnorm[here, :] = jnp.sum(wide * wide, axis=1, keepdims=True)
    low = low_lanes()
    rows = []
    for i in range(n):
        cols = slice(i * PIECE, (i + 1) * PIECE)
        top, total = [], []
        for j in range(2):
            here = slice(j * HALF, (j + 1) * HALF)
            cross = lax.dot_general(
                cent[here, :],
                pts[i][...],
                (((1,), (1,)), ((), ())),
                preferred_element_type=jnp.float32,
            )
            part = (2.0 * cross - cnorm[here, :]) * SCALE
            top.append(jnp.max(part, axis=0, keepdims=True))
            part = jnp.exp(part - top[j])
            weights[j][:, cols] = part
            tops[j : j + 1, cols] = top[j]
            total.append(jnp.sum(part, axis=0, keepdims=True))
        peak = jnp.maximum(top[0], top[1])
        whole = total[0] * jnp.exp(top[0] - peak) + total[1] * jnp.exp(top[1] - peak)
        logs = peak + jnp.log(whole)
        for h in range(2):
            rows.append(logs[:, h * 128 : (h + 1) * 128])
    if not prior:
        for i, row in enumerate(rows):
            out[i : i + 1, :] = row
    else:
        all_rows = [b[i : i + 1, :] for b in before for i in range(b.shape[0])] + rows
        for i, row in enumerate(all_rows):
            straight = jnp.broadcast_to(row, (8, 128))
            turned = pltpu.roll(straight, UNIT, 1)
            for h in range(2):
                unit = units[2 * i + h]
                a = unit[0] == "a"
                value = straight if (h == 0) == a else turned
                lanes = slice(0, UNIT) if a else slice(UNIT, 128)
                place[pl.ds(block_of(unit, pos[0], pos[1]), 1), lanes] = value[0:1, lanes]
        whole = place[:BLOCKS, :]
        for j in range(N_CENT):
            out[j] = whole


def local_weights(pos, centroids, pts, cnorm=None, before=()):
    m = len(pts)
    n = m // 2 if before else m
    units = sum(PIECES, ()) if cnorm is not None else ()
    stats = f32(N_CENT, BLOCKS, 128) if before else f32(2 * n, 128)
    args = (centroids, *pts, *before) + (() if cnorm is None else (cnorm,))
    outs = (stats,) + ((f32(K_DEV, 1),) if cnorm is None else ())
    if before:
        outs = (bf16(PIECE, D), bf16(PIECE, D), stats)
    outs += (f32(HALF, n * PIECE), f32(HALF, n * PIECE), f32(2, n * PIECE))
    return call(
        functools.partial(logits_body, m, units, len(before)),
        "weights",
        pos,
        args,
        outs,
        [pltpu.VMEM((BLOCKS + 8, 128), jnp.float32)] if before else [],
        flops=2 * K_DEV * n * PIECE * D,
        exps=K_DEV * n * PIECE,
    )


def merge_stats(pos, every, tops, place, turned, rows):
    low = low_lanes()[0:1]
    peak = every[0]
    for j in range(1, N_CENT):
        peak = jnp.maximum(peak, every[j])
    total = jnp.zeros_like(peak)
    for j in range(N_CENT):
        total = total + jnp.exp(every[j] - peak)
    both = []
    for value in (peak, 1.0 / total):
        place[:BLOCKS, :] = value
        turned[:BLOCKS, :] = pltpu.roll(value, UNIT, 1)
        parts = []
        for units in PIECES:
            for h in range(2):
                pair = units[2 * h : 2 * h + 2]
                refs = (place, turned) if pair[0][0] == "a" else (turned, place)
                first, second = (
                    ref[pl.ds(block_of(unit, pos[0], pos[1]), 1), :]
                    for ref, unit in zip(refs, pair)
                )
                parts.append(jnp.where(low, first, second))
        both.append(parts)
    at = 0
    for ref in tops:
        for h in range(ref.shape[1] // 128):
            lanes = slice(h * 128, (h + 1) * 128)
            rows[0:2, at * 128 : (at + 1) * 128] = jnp.exp(ref[:, lanes] - both[0][at]) * both[1][at]
            at += 1
    return peak + jnp.log(total)


def columns(pos, which):
    return pl.ds(pl.multiple_of(pos[which] * WIDTH, WIDTH), WIDTH)


def sums_body(chunk, pos, *refs):
    weights, pts, refs = refs[:3], refs[3:11], refs[11:]
    if chunk == 0:
        every, tops, sums = refs[0], refs[1:4], refs[4:8]
        partition, rows, resp, place, turned = refs[8:]
        partition[...] = merge_stats(pos, every, tops, place, turned, rows)
    else:
        rows, sums, resp = refs[0], refs[1:5], refs[5]
    cnt, p = None, 0
    for ref in weights:
        for j in range(ref.shape[1] // PIECE):
            here = slice(p * PIECE, (p + 1) * PIECE)
            part = ref[:, j * PIECE : (j + 1) * PIECE]
            r = (part * rows[chunk : chunk + 1, here]).astype(jnp.bfloat16)
            resp[:, here] = r
            wide = r.astype(jnp.float32)
            two = wide[:, :128] + wide[:, 128:]
            cnt = cnt + two if p else two
            p += 1
    for k in range(4):
        acc = None
        for p in range(8):
            d = jnp.dot(
                resp[:, p * PIECE : (p + 1) * PIECE],
                pts[p][:, columns(pos, 2 + k)],
                preferred_element_type=jnp.float32,
            )
            acc = acc + d if p else d
        sums[k][:, :WIDTH] = acc
    sums[0][:, WIDTH:] = jnp.broadcast_to(jnp.sum(cnt, axis=1, keepdims=True), (HALF, 128))


def chunk_sums(pos, chunk, weights, pts, stats):
    outs = [f32(HALF, WIDTH + 128)] + [f32(HALF, WIDTH)] * 3
    scratch = [pltpu.VMEM((HALF, ROWS), jnp.bfloat16)]
    if chunk == 0:
        outs += [f32(BLOCKS, 128), f32(8, ROWS)]
        scratch += [pltpu.VMEM((BLOCKS + 8, 128), jnp.float32)] * 2
    return call(
        functools.partial(sums_body, chunk),
        "sums",
        pos,
        (*weights, *pts, *stats),
        outs,
        scratch,
        flops=2 * HALF * ROWS * D,
    )


def one_hot(shape):
    return (lax.broadcasted_iota(jnp.int32, shape, 0) == 0).astype(jnp.float32)


def pack_body(pos, first, second, got, *refs):
    packed, counts, row = refs[-3:]
    cnt = first[:, WIDTH:] + got[:, WIDTH:]
    counts[...] = cnt
    here = lax.dot_general(
        one_hot((128, 8)),
        cnt,
        (((0,), (1,)), ((), ())),
        precision=lax.Precision.HIGHEST,
        preferred_element_type=jnp.float32,
    )
    if len(refs) > 3:
        row[:8, :] = refs[0][...]
        row[8:, :] = here
    else:
        row[...] = here
    factor = SPAN / (cnt + 0.25)
    for k in range(2):
        lanes = slice(k * 128, (k + 1) * 128)
        packed[:, lanes] = (second[:, lanes] + got[:, lanes]) * factor


def pack(pos, first, second, got, after, before=()):
    outs = (f32(HALF, WIDTH), f32(HALF, 128), f32(16 if before else 8, HALF))
    return call(pack_body, "pack", pos, (first, second, got, *before), outs, after=after)


def near_body(pos, *refs):
    cent, near = refs[4:]
    for c in range(2):
        here = slice(c * HALF, (c + 1) * HALF)
        for k in range(2):
            lanes = slice(k * 128, (k + 1) * 128)
            own = cent[here, pl.ds(pl.multiple_of(pos[6] * WIDTH + k * 128, 128), 128)]
            total = refs[c][:, lanes] + refs[2 + c][:, lanes]
            near[here, lanes] = total + 0.25 * own.astype(jnp.float32)


def fresh_body(pos, near, counts0, counts1, far_row, far0, far1, out):
    for c, (counts, far) in enumerate(((counts0, far0), (counts1, far1))):
        here = slice(c * HALF, (c + 1) * HALF)
        far_counts = lax.dot_general(
            far_row[8 * c : 8 * (c + 1), :],
            one_hot((8, 128)),
            (((0,), (0,)), ((), ())),
            precision=lax.Precision.HIGHEST,
            preferred_element_type=jnp.float32,
        )
        weight = 1.0 / (counts[...] + far_counts + 0.25)
        factor = (far_counts + 0.25) * (1.0 / SPAN)
        for k in range(2):
            lanes = slice(k * 128, (k + 1) * 128)
            total = near[here, lanes] + far[:, lanes] * factor
            out[here, lanes] = (total * weight).astype(out.dtype)


FROM_PAIR = [(i, i ^ 1) for i in range(N_CENT)]


def from_x(d):
    return [(i, i ^ 2 * d) for i in range(N_CENT)]


def from_z(d):
    return [(i, i ^ 8 * d) for i in range(N_CENT)]


TO_CORE = [(i, i ^ 1) for i in range(4)]
TO_Y = [(i, i ^ 2) for i in range(4)]


def on_device(points, centroids):
    dp, cent = lax.axis_index("dp"), lax.axis_index("cent")
    core, y_hi = dp % 2, dp // 2
    z, x, y_lo = cent // 8, cent // 2 % 4, cent % 2
    far, near = 2 * (1 - y_hi), 2 * y_hi
    pos = jnp.stack([z, x, far + 1 - core, far + core, near + 1 - core, near + core, dp])

    other = lax.ppermute(points, "cent", FROM_PAIR)
    half = PTS_DEV // 2
    first = jnp.where(y_lo == 0, points, other)
    second = jnp.where(y_lo == 0, other, points)
    a = jnp.concatenate([first[:half], second[:half]])
    b = jnp.concatenate([first[half:], second[half:]])
    a4, b4 = join(
        pos,
        [a] + [lax.ppermute(a, "cent", from_x(d)) for d in STEPS[1:]],
        [b] + [lax.ppermute(b, "cent", from_z(d)) for d in STEPS[1:]],
    )
    a1, b1 = lax.ppermute(a4, "cent", from_z(1)), lax.ppermute(b4, "cent", from_x(1))
    a3, b3 = lax.ppermute(a4, "cent", from_z(3)), lax.ppermute(b4, "cent", from_x(3))
    mid = PIECE // 2
    last = [
        lax.ppermute(a3[:mid], "cent", from_z(1)),
        lax.ppermute(a1[mid:], "cent", from_z(3)),
        lax.ppermute(b3[:mid], "cent", from_x(1)),
        lax.ppermute(b1[mid:], "cent", from_x(3)),
    ]
    pts = [a4, b4, a1, a3, b1, b3]

    st0, cnorm, *w0, top0 = local_weights(pos, centroids, pts[:2])
    st1, *w1, top1 = local_weights(pos, centroids, pts[2:6], cnorm)
    a2, b2, stats, *w2, top2 = local_weights(pos, centroids, last, cnorm, (st0, st1))
    pts += [a2, b2]

    every = lax.all_to_all(stats, "cent", 0, 0)

    weights = list(zip(w0, w1, w2))
    *sums0, partition, rows = chunk_sums(pos, 0, weights[0], pts, (every, top0, top1, top2))
    sums1 = chunk_sums(pos, 1, weights[1], pts, (rows,))
    got0 = lax.ppermute(sums0[0], "dp", TO_CORE)
    got1 = lax.ppermute(sums1[0], "dp", TO_CORE)
    packed0, counts0, row = pack(pos, sums0[0], sums0[1], got0, (sums1[0],))
    packed1, counts1, row = pack(pos, sums1[0], sums1[1], got1, (), (row,))
    far = [lax.ppermute(p.astype(jnp.float16), "dp", TO_Y) for p in (packed0, packed1)]
    far_row = lax.ppermute(row, "dp", TO_Y)

    near_got = [lax.ppermute(s[2], "dp", TO_CORE) for s in (sums0, sums1)]
    (near,) = call(
        near_body,
        "near",
        pos,
        (sums0[3], sums1[3], *near_got, centroids),
        (f32(K_DEV, WIDTH),),
        after=(packed1,),
    )
    far = [f.astype(jnp.float32) for f in far]
    args = (near, counts0, counts1, far_row, *far)
    (fresh,) = call(fresh_body, "fresh", pos, args, (bf16(K_DEV, WIDTH),))

    mine = 4 * z + x
    own_rows = jnp.concatenate(
        [
            lax.dynamic_slice(partition, (mine, y_lo * half + UNIT * i), (1, half))[0]
            for i in range(2)
        ]
    )
    return fresh, own_rows


def solution(mesh):
    placed = (P(("dp", "cent"), None), P("cent", None))
    return jax.shard_map(
        on_device,
        mesh=mesh,
        in_specs=placed,
        out_specs=(P("cent", "dp"), P(("dp", "cent"))),
        check_vma=False,
    )
```
